32 devices in a mesh: groups: 2 (over y), space: 8 (over z, x), tm: 2 (over core).
Axes of the slice: x: 2, y: 2, z: 4, core: 2. Of those that a mesh axis runs over, the one named last changes fastest.
Arguments:
- incr: bfloat16 [16, 64, 8192], P(('groups', 'tm'), None, 'space'), parts along dimension 0, may hold values from -6 to 6
- costate: bfloat16 [16, 64, 8192], P(('groups', 'tm'), None, 'space'), parts along dimension 0, may hold values from -6 to 6
- lateral_mix: bfloat16 [9, 128, 128], replicated, may hold values from -0.5 to 0.5
- vertical_mix: bfloat16 [9, 64, 64], replicated, may hold values from -0.75 to 0.75
- neighbours: int32 [128, 9], P(('groups', 'space')), parts along dimension 0, may hold values from 0 to 63, as said below
- obs_lateral: bfloat16 [16, 128, 2048], P(('groups', 'tm'), None, 'space'), parts along dimension 0, may hold values from -0.5 to 0.5
- obs_vertical: bfloat16 [16, 64, 2048], P(('groups', 'tm'), None, 'space'), parts along dimension 0, may hold values from -0.75 to 0.75
- obs_weight: bfloat16 [16, 2048], P(('groups', 'tm'), 'space'), parts along dimension 0, may hold values from -24 to 24
- obs_block: int32 [16, 2048], P(('groups', 'tm'), 'space'), parts along dimension 0, may hold values from 0 to 7
- obs_count: int32 [16, 64], P(('groups', 'tm'), 'space'), parts along dimension 0, may hold values from 0 to 32, as said below
Outputs:
- model_residual: bfloat16 [16, 64, 8192], P(('groups', 'tm'), None, 'space'), parts along dimension 0
- adjoint_image: bfloat16 [16, 64, 8192], P(('groups', 'tm'), None, 'space'), parts along dimension 0
- obs_image: float32 [16, 2048], P(('groups', 'tm'), 'space'), parts along dimension 0
The draws below stay inside these ranges and needn't reach their ends.
There are 2 independent parts, one for each index of `groups`. The reference program is written for one: setup_inputs(seed, part) draws one part's arguments, and reference() takes and returns one part's arrays. A program takes and returns all parts, laid end to end along the dimension named above; an argument that names none is the same for every part. Nothing has to cross between parts.
Inputs may be any that keep to these rules, and one draw needn't show every extreme that they name: `neighbours`: row b names blocks within 2 of b inside the grid; in one entry of each row the distance is exactly 2 unless the grid's end clips it. `obs_count`: in every subwindow one tile, drawn from the seed, has 32 live slots from every holder.
All inputs are finite; a program needn't handle non-finite values.
Results may differ from the reference program's by a relative error of at most 0.0047.
Values may be sent and summed in bfloat16 or wider, within the bound.
No kernel may reach another device: no remote copies, remote signals or barrier semaphores. Data moves between devices by JAX's collectives and lax.ppermute only.
A program may use at most 128 MiB of HBM per device.

```python
import jax
import jax.numpy as jnp
from jax import lax

LEV = 64
BLOCK = 128
NBR = 9
REACH = 2
SUB = 8
BLK_DEV = 8
OBS_DEV = 256
TILES = 8
NBLK = 64
COLS = 8192
NOBS = 2048
CAP = 32


def draw_neighbours(key, part):
    key = jax.random.fold_in(key, 11)
    first, second, third = jax.random.split(key, 3)
    offsets = jax.random.randint(first, (NBLK, NBR), -REACH, REACH + 1)
    column = jax.random.randint(second, (NBLK, 1), 0, NBR)
    side = jax.random.randint(third, (NBLK, 1), 0, 2) * 2 - 1
    offsets = jnp.where(jnp.arange(NBR)[None, :] == column, side * REACH, offsets)
    block_ids = jnp.arange(NBLK)[:, None] + offsets
    return jnp.clip(block_ids, 0, NBLK - 1).astype(jnp.int32)


def draw_obs_count(key, part):
    key = jax.random.fold_in(key, 17)
    first, second = jax.random.split(key)
    counts = jax.random.randint(first, (SUB, TILES, TILES), 0, CAP + 1)
    chosen = jax.random.randint(second, (SUB, 1, 1), 0, TILES)
    counts = jnp.where(jnp.arange(TILES)[None, :, None] == chosen, CAP, counts)
    return counts.reshape(SUB, TILES * TILES).astype(jnp.int32)


def set_ends(array, key, low, top_value):
    index_at = [jax.random.randint(jax.random.fold_in(key, axis), (), 0, length) for axis, length in enumerate(array.shape)]
    longest = array.shape.index(max(array.shape))
    beside = index_at[:longest] + [(index_at[longest] + 1) % array.shape[longest]] + index_at[longest + 1:]
    return array.at[tuple(index_at)].set(low).at[tuple(beside)].set(top_value)


def block_scale(stream_key, extent, shards, low, top_value):
    gain, own = 1.0, jax.random.fold_in(stream_key, 6)
    for axis_at, shards_of in shards:
        heights = jnp.exp(jax.random.uniform(jax.random.fold_in(own, axis_at), (shards_of,), jnp.float32, low / len(shards), top_value / len(shards)))
        gain = gain * jnp.repeat(heights, extent[axis_at] // shards_of).reshape([-1 if axis == axis_at else 1 for axis in range(len(extent))])
    return gain


def centred(stream_key, dims, deviation, reach, shards=(), held_as=jnp.bfloat16):
    level = block_scale(stream_key, dims, shards, -0.22, 0.18) if shards else 1.0
    values = jax.random.normal(stream_key, dims, jnp.float32) * deviation * level
    return jnp.minimum(jnp.maximum(values, -reach), reach).astype(held_as)


def setup_inputs(seed: int = 0, part: int = 0) -> dict:
    key_of = jax.random.split(jax.random.key(seed), 11)
    own_keys = jax.random.split(jax.random.fold_in(key_of[10], part), 11)
    return {
        "incr": centred(own_keys[0], (SUB, LEV, COLS), 1.0, 6.0, ((0, 2), (2, 8))),
        "costate": centred(own_keys[1], (SUB, LEV, COLS), 1.0, 6.0, ((0, 2), (2, 8))),
        "lateral_mix": centred(key_of[2], (NBR, BLOCK, BLOCK), BLOCK ** -0.5, 0.5),
        "vertical_mix": centred(key_of[3], (NBR, LEV, LEV), LEV ** -0.5, 0.75),
        "neighbours": draw_neighbours(jax.random.fold_in(jax.random.fold_in(key_of[10], part), 71), part),
        "obs_lateral": centred(own_keys[5], (SUB, BLOCK, NOBS), BLOCK ** -0.5, 0.5, ((0, 2), (2, 8))),
        "obs_vertical": centred(own_keys[6], (SUB, LEV, NOBS), LEV ** -0.5, 0.75, ((0, 2), (2, 8))),
        "obs_weight": centred(own_keys[7], (SUB, NOBS), 4.0, 24.0, ((0, 2), (1, 8))),
        "obs_block": set_ends(jax.random.randint(own_keys[8], (SUB, NOBS), 0, BLK_DEV), jax.random.fold_in(own_keys[8], 1), 0, BLK_DEV - 1).astype(jnp.int32),
        "obs_count": draw_obs_count(jax.random.fold_in(jax.random.fold_in(key_of[10], part), 71), part),
    }


def mix_tile(blocks, block_index, lateral_mix, vertical_mix):
    gathered = jnp.take(blocks, block_index, axis=1).astype(jnp.float32)
    lateral = jnp.einsum('lbjc,jcd->lbjd', gathered, lateral_mix.astype(jnp.float32)).astype(jnp.bfloat16)
    return jnp.einsum('jml,lbjd->mbd', vertical_mix.astype(jnp.float32), lateral.astype(jnp.float32))


def forward_field(field, neighbours, lateral_mix, vertical_mix):
    margin = REACH * BLOCK
    padded = jnp.pad(field, ((0, 0), (margin, margin)))
    blocks = padded.reshape(LEV, NBLK + 2 * REACH, BLOCK)

    def one_tile(tile):
        block_index = lax.dynamic_slice_in_dim(neighbours, tile * BLK_DEV, BLK_DEV, 0) + REACH
        return mix_tile(blocks, block_index, lateral_mix, vertical_mix)

    pushed = lax.map(one_tile, jnp.arange(TILES, dtype=jnp.int32))
    return jnp.transpose(pushed, (1, 0, 2, 3)).reshape(LEV, COLS)


def backward_field(field, neighbours, lateral_mix, vertical_mix):
    blocks = field.reshape(LEV, NBLK, BLOCK)

    def one_tile(total, tile):
        source = lax.dynamic_slice_in_dim(blocks, tile * BLK_DEV, BLK_DEV, 1).astype(jnp.float32)
        block_index = lax.dynamic_slice_in_dim(neighbours, tile * BLK_DEV, BLK_DEV, 0) + REACH
        back = jnp.einsum('jml,mbd->lbjd', vertical_mix.astype(jnp.float32), source).astype(jnp.bfloat16)
        contributions = jnp.einsum('lbjd,jcd->lbjc', back.astype(jnp.float32), lateral_mix.astype(jnp.float32))
        return total.at[:, block_index].add(contributions), None

    start = jnp.zeros((LEV, NBLK + 2 * REACH, BLOCK), jnp.float32)
    total, unused = lax.scan(one_tile, start, jnp.arange(TILES, dtype=jnp.int32))
    return total[:, REACH:REACH + NBLK].reshape(LEV, COLS)


def observe_window(field, lateral, vertical, weight, owner_block, counts):
    lateral_own = jnp.transpose(lateral.reshape(BLOCK, TILES, TILES, CAP), (2, 0, 1, 3)).reshape(TILES, BLOCK, OBS_DEV)
    vertical_own = jnp.transpose(vertical.reshape(LEV, TILES, TILES, CAP), (2, 0, 1, 3)).reshape(TILES, LEV, OBS_DEV)
    weight_own = jnp.transpose(weight.reshape(TILES, TILES, CAP), (1, 0, 2)).reshape(TILES, OBS_DEV)
    live_slot = (jnp.arange(CAP, dtype=jnp.int32)[None, None, :] < counts.reshape(TILES, TILES)[:, :, None])
    live_slot = live_slot.reshape(TILES, OBS_DEV)
    global_block = owner_block.reshape(TILES, OBS_DEV) + (jnp.arange(TILES, dtype=jnp.int32) * BLK_DEV)[:, None]
    blocks = field.reshape(LEV, NBLK, BLOCK)

    def one_tile(total, pieces):
        footprint, weighting, multiplier, block_ids, alive = pieces
        alive_float = alive.astype(jnp.float32)
        picked = jnp.take(blocks, block_ids, axis=1).astype(jnp.float32)
        along = jnp.sum(picked * jnp.transpose(footprint).astype(jnp.float32)[None], axis=2)
        observed = alive_float * jnp.sum(weighting.astype(jnp.float32) * along, axis=0)
        scaled = (multiplier.astype(jnp.float32)[None, :] * weighting.astype(jnp.float32)).astype(jnp.bfloat16)
        masked = scaled.astype(jnp.float32) * alive_float[None, :]
        contributions = masked[:, :, None] * jnp.transpose(footprint).astype(jnp.float32)[None]
        return total.at[:, block_ids].add(contributions), observed

    start = jnp.zeros((LEV, NBLK, BLOCK), jnp.float32)
    total, observed = lax.scan(one_tile, start, (lateral_own, vertical_own, weight_own, global_block, live_slot))
    return observed.reshape(NOBS), total.reshape(LEV, COLS)


def reference(incr, costate, lateral_mix, vertical_mix, neighbours, obs_lateral, obs_vertical, obs_weight, obs_block, obs_count):
    residual_list = []
    adjoint_list = []
    image_list = []
    pulled = [backward_field(costate[moment], neighbours, lateral_mix, vertical_mix) for moment in range(1, SUB)]
    for moment in range(SUB):
        if moment == 0:
            pushed = jnp.zeros((LEV, COLS), jnp.float32)
        else:
            pushed = forward_field(incr[moment - 1], neighbours, lateral_mix, vertical_mix)
        residual_list.append((incr[moment].astype(jnp.float32) - pushed).astype(jnp.bfloat16))
        observed, obs_push = observe_window(incr[moment], obs_lateral[moment], obs_vertical[moment], obs_weight[moment], obs_block[moment], obs_count[moment])
        image_list.append(observed)
        total = costate[moment].astype(jnp.float32) + obs_push
        if moment + 1 < SUB:
            total = total - pulled[moment]
        adjoint_list.append(total.astype(jnp.bfloat16))
    return jnp.stack(residual_list), jnp.stack(adjoint_list), jnp.stack(image_list)
```

```python
import functools

import jax
import jax.numpy as jnp
from jax import lax
from jax.experimental import pallas as pl
from jax.experimental.pallas import tpu as pltpu
from jax.sharding import PartitionSpec as P

REACH = 2
ROW_TILE = 16
BF16 = jnp.bfloat16
F32 = jnp.float32
VMEM = pl.BlockSpec(memory_space=pltpu.VMEM)
SMEM = pl.BlockSpec(memory_space=pltpu.SMEM)


def dot(a, b):
    return jnp.dot(a, b, preferred_element_type=F32)


def dot_nt(a, b):
    return lax.dot_general(a, b, (((1,), (1,)), ((), ())), preferred_element_type=F32)


def exchanged(array, pairs):
    both = [(a, b) for a, b in pairs] + [(b, a) for a, b in pairs]
    return lax.ppermute(array, "space", both)


def call(kernel, out_shape, args, specs, scratch=(), flops=0, moved=0, limit=None):
    multiple = isinstance(out_shape, (list, tuple))
    return pl.pallas_call(
        kernel,
        out_shape=out_shape,
        in_specs=specs,
        out_specs=[VMEM] * len(out_shape) if multiple else VMEM,
        scratch_shapes=list(scratch),
        compiler_params=pltpu.CompilerParams(vmem_limit_bytes=limit or 48 * 1024 * 1024),
        cost_estimate=pl.CostEstimate(flops=flops, bytes_accessed=moved, transcendentals=0),
    )(*args)


def pack_kernel(obs_lateral, obs_vertical, obs_weight, out):
    moments, cols, slots = obs_lateral.shape
    levels = obs_vertical.shape[1]
    tiles = out.shape[0]
    cap = slots // tiles
    tail = out.shape[1] - cols - levels
    for tile in range(tiles):
        lanes = slice(tile * cap, (tile + 1) * cap)
        out[tile, :cols] = jnp.concatenate([obs_lateral[s, :, lanes] for s in range(moments)], axis=1)
        out[tile, cols : cols + levels] = jnp.concatenate(
            [obs_vertical[s, :, lanes] for s in range(moments)], axis=1
        )
        row = jnp.concatenate([obs_weight[s : s + 1, lanes].astype(F32) for s in range(moments)], axis=1)
        out[tile, cols + levels :] = jnp.broadcast_to(row, (tail, row.shape[1])).astype(BF16)


def halo_kernel(info, incr, costate, crossed, neighbours, first, second):
    moments, levels, cols = incr.shape
    blocks = neighbours.shape[0]
    width = first.shape[1]
    odd = info[0]
    anchor = info[2]
    near = cols - width
    for target, lane in ((first, (1 - odd) * near), (second, odd * near)):
        lanes = pl.ds(pl.multiple_of(lane, 128), width)
        for k in range(moments - 1):
            target[k * levels : (k + 1) * levels] = incr[k, :, lanes]
            base = (moments - 1 + k) * levels
            target[base : base + levels] = costate[k + 1, :, lanes]
        base = 2 * (moments - 1) * levels
        target[base : base + levels] = crossed[:, lanes]
        base += levels
        own = lax.broadcasted_iota(jnp.int32, (blocks, neighbours.shape[1]), 0) + anchor
        offset = (neighbours[...] - own).astype(F32)
        target[base:] = jnp.zeros((target.shape[0] - base, width), BF16)
        tile = jnp.concatenate([offset, jnp.zeros((target.shape[0] - base - blocks, offset.shape[1]), F32)], axis=0)
        target[base:, : offset.shape[1]] = tile.astype(BF16)


def prepare_kernel(lateral_mix, vertical_mix, pair_fwd, pair_bwd, vert_fwd, vert_bwd):
    entries, cols, _ = lateral_mix.shape
    levels = vertical_mix.shape[1]
    pair_fwd[...] = jnp.zeros(pair_fwd.shape, BF16)
    pair_bwd[...] = jnp.zeros(pair_bwd.shape, BF16)
    for j in range(entries):
        at = slice((j % 2) * cols, (j % 2 + 1) * cols)
        pair_fwd[j // 2, at, at] = lateral_mix[j]
        pair_bwd[j // 2, at, at] = lateral_mix[j].astype(F32).T.astype(BF16)
    vert_fwd[...] = jnp.concatenate([vertical_mix[j] for j in range(entries)], axis=1)
    vert_bwd[...] = jnp.concatenate([vertical_mix[j].astype(F32).T.astype(BF16) for j in range(entries)], axis=1)


def mixed(get, count, blocks, entries, pair, vert, stage):
    levels = vert.shape[0]
    cols = pair.shape[1] // 2
    for k in range((entries + 1) // 2):
        single = 2 * k + 1 >= entries
        weight = pair[k, :cols, :cols] if single else pair[k]
        for s in range(count):
            rows = []
            for b in blocks:
                part = get(s, b, 2 * k)
                rows.append(part if single else jnp.concatenate([part, get(s, b, 2 * k + 1)], axis=1))
            result = dot(jnp.concatenate(rows, axis=0), weight).astype(BF16)
            for i in range(len(blocks)):
                piece = result[i * levels : (i + 1) * levels]
                lanes = slice(i * cols, (i + 1) * cols)
                stage[s, 2 * k * levels : (2 * k + 1) * levels, lanes] = piece[:, :cols]
                if not single:
                    stage[s, (2 * k + 1) * levels : (2 * k + 2) * levels, lanes] = piece[:, cols:]
    return [dot(vert[...], stage[s]) for s in range(count)]


def interior_kernel(
    info, near, incr, costate, crossed, pair_fwd, pair_bwd, vert_fwd, vert_bwd, residual, pulled, before, after, stage
):
    moments, levels, cols_all = incr.shape
    blocks, entries = near.shape
    cols = cols_all // blocks
    inner = list(range(REACH, blocks - REACH))
    lanes = slice(REACH * cols, (blocks - REACH) * cols)
    tm = info[1]
    anchor = info[2]
    gate = tm.astype(F32)
    before[...] = (crossed[...].astype(F32) * gate).astype(BF16)
    after[...] = (crossed[...].astype(F32) * (1.0 - gate)).astype(BF16)

    def forward(s, b, j):
        at = pl.ds(pl.multiple_of((near[b, j] - anchor) * cols, cols), cols)
        return before[:, at] if s == 0 else incr[s - 1, :, at]

    for s, pushed in enumerate(mixed(forward, moments, inner, entries, pair_fwd, vert_fwd, stage)):
        residual[s] = (incr[s, :, lanes].astype(F32) - pushed).astype(BF16)

    def backward(s, n, j):
        total = None
        for b in range(n - REACH, n + REACH + 1):
            at = slice(b * cols, (b + 1) * cols)
            source = after[:, at] if s == moments - 1 else costate[s + 1, :, at]
            term = jnp.where(near[b, j] == anchor + n, source, jnp.zeros_like(source))
            total = term if total is None else total + term
        return total

    for s, value in enumerate(mixed(backward, moments, inner, entries, pair_bwd, vert_bwd, stage)):
        pulled[s] = value


def final_kernel(
    packed, info, near, counts, incr, costate, crossed, first, second, arrived, owner,
    pair_fwd, pair_bwd, vert_fwd, vert_bwd, inner_residual, inner_pulled,
    residual, adjoint, image, before, after, stage, pulled, masked,
):
    moments, levels, cols_all = incr.shape
    blocks, entries = near.shape
    cols = cols_all // blocks
    width = REACH * cols
    odd = info[0]
    tm = info[1]
    anchor = info[2]
    gate = tm.astype(F32)
    outer = [b for b in range(blocks) if b < REACH or b >= blocks - REACH]
    inner_lanes = slice(width, cols_all - width)

    own = slice(width, width + cols_all)
    for s in range(moments):
        edge = 2 * (moments - 1) * levels if s == 0 else (s - 1) * levels
        if s == 0:
            before[s, :, own] = (crossed[...].astype(F32) * gate).astype(BF16)
        else:
            before[s, :, own] = incr[s - 1]
        rows = slice(edge, edge + levels)
        one, two = first[rows], second[rows]
        if s == 0:
            one, two = (one.astype(F32) * gate).astype(BF16), (two.astype(F32) * gate).astype(BF16)
        before[s, :, :width] = jnp.where(odd == 1, one, two)
        before[s, :, width + cols_all :] = jnp.where(odd == 1, two, one)
        last = s == moments - 1
        edge = (moments - 1 + (moments - 1 if last else s)) * levels
        rows = slice(edge, edge + levels)
        one, two = first[rows], second[rows]
        if last:
            one, two = (one.astype(F32) * (1.0 - gate)).astype(BF16), (two.astype(F32) * (1.0 - gate)).astype(BF16)
            after[s, :, own] = (crossed[...].astype(F32) * (1.0 - gate)).astype(BF16)
        else:
            after[s, :, own] = costate[s + 1]
        after[s, :, :width] = jnp.where(odd == 1, one, two)
        after[s, :, width + cols_all :] = jnp.where(odd == 1, two, one)

    def forward(s, b, j):
        at = pl.ds(pl.multiple_of((near[b, j] - anchor + REACH) * cols, cols), cols)
        return before[s, :, at]

    for s, pushed in enumerate(mixed(forward, moments, outer, entries, pair_fwd, vert_fwd, stage)):
        residual[s, :, :width] = (incr[s, :, :width].astype(F32) - pushed[:, :width]).astype(BF16)
        residual[s, :, inner_lanes] = inner_residual[s]
        residual[s, :, cols_all - width :] = (
            incr[s, :, cols_all - width :].astype(F32) - pushed[:, width:]
        ).astype(BF16)

    base = (2 * moments - 1) * levels
    one, two = first[base : base + ROW_TILE, :cols].astype(F32), second[base : base + ROW_TILE, :cols].astype(F32)
    left = jnp.where(odd == 1, one, two)
    right = jnp.where(odd == 1, two, one)

    def backward(s, n, j):
        total = None
        for b in range(n - REACH, n + REACH + 1):
            source = after[s, :, (b + REACH) * cols : (b + REACH + 1) * cols]
            if 0 <= b < blocks:
                term = jnp.where(near[b, j] == anchor + n, source, jnp.zeros_like(source))
            else:
                row = b + blocks if b < 0 else b - blocks
                offset = (left if b < 0 else right)[row : row + 1, j : j + 1]
                hit = jnp.where(offset == float(n - b), 1.0, 0.0)
                term = source * jnp.broadcast_to(hit, source.shape).astype(BF16)
            total = term if total is None else total + term
        return total

    for s, value in enumerate(mixed(backward, moments, outer, entries, pair_bwd, vert_bwd, stage)):
        pulled[s] = value

    tiles = counts.shape[1]
    slots = owner.shape[1]
    cap = slots // tiles
    slot = lax.broadcasted_iota(jnp.int32, (1, slots), 1)
    for s in range(moments):
        limit = jnp.zeros((1, slots), jnp.int32)
        for h in range(tiles):
            inside = (slot >= h * cap) & (slot < h * cap + counts[s, h])
            limit = jnp.where(inside, 1, limit)
        block = jnp.where(limit == 1, owner[s : s + 1], -1)
        if packed:
            part = slice(s * cap, (s + 1) * cap)
            whole = jnp.concatenate([arrived[h, :, part] for h in range(tiles)], axis=1)
        else:
            whole = arrived[s]
        lateral = whole[:cols]
        vertical = whole[cols : cols + levels].astype(F32)
        weight = whole[cols + levels : cols + levels + ROW_TILE].astype(F32)[:1]
        for b in range(blocks):
            hit = jnp.where(block == b, 1.0, 0.0)
            masked[b * cols : (b + 1) * cols] = lateral * jnp.broadcast_to(hit, lateral.shape).astype(BF16)
        along = dot(incr[s], masked[...])
        image[s : s + 1] = jnp.sum(vertical * along, axis=0, keepdims=True)
        scaled = (vertical * weight).astype(BF16)
        total = costate[s].astype(F32) + dot_nt(scaled, masked[...])
        adjoint[s, :, :width] = (total[:, :width] - pulled[s, :, :width]).astype(BF16)
        adjoint[s, :, inner_lanes] = (total[:, inner_lanes] - inner_pulled[s]).astype(BF16)
        adjoint[s, :, cols_all - width :] = (total[:, cols_all - width :] - pulled[s, :, width:]).astype(BF16)


def on_device(
    incr, costate, lateral_mix, vertical_mix, neighbours,
    obs_lateral, obs_vertical, obs_weight, obs_block, obs_count,
):
    moments, levels, cols_all = incr.shape
    entries, cols, _ = lateral_mix.shape
    blocks = neighbours.shape[0]
    slots = obs_block.shape[1]
    tiles = lax.axis_size("space")
    cap = slots // tiles
    width = REACH * cols
    place = lax.axis_index("space")
    tm = lax.axis_index("tm")
    info = jnp.stack([place % 2, tm, place * blocks]).astype(jnp.int32)
    shape = jax.ShapeDtypeStruct

    crossing = jnp.where(tm == 0, incr[-1], costate[0])
    crossed = lax.ppermute(crossing, "tm", [(0, 1), (1, 0)])

    height = cols + levels + ROW_TILE
    packed = moments * cap == 128
    if packed:
        outgoing = call(
            pack_kernel,
            shape((tiles, height, moments * cap), BF16),
            (obs_lateral, obs_vertical, obs_weight),
            [VMEM] * 3,
            moved=1 << 20,
        )
    else:
        stacked = jnp.concatenate(
            [obs_lateral, obs_vertical, jnp.broadcast_to(obs_weight[:, None], (moments, ROW_TILE, slots))], axis=1
        )
        outgoing = stacked.reshape(moments, height, tiles, cap).transpose(2, 1, 0, 3).reshape(tiles, height, -1)

    halo = shape(((2 * moments - 1) * levels + ROW_TILE, width), BF16)
    first, second = call(
        halo_kernel, [halo, halo], (info, incr, costate, crossed, neighbours), [SMEM] + [VMEM] * 4, moved=1 << 20
    )
    first = exchanged(first, [(i, i + 1) for i in range(0, tiles - 1, 2)])
    second = exchanged(second, [(i, i + 1) for i in range(1, tiles - 1, 2)])

    arrived = lax.all_to_all(outgoing, "space", split_axis=0, concat_axis=0, tiled=True)
    if not packed:
        arrived = arrived.reshape(tiles, height, moments, cap).transpose(2, 1, 0, 3).reshape(moments, height, slots)

    pairs = (entries + 1) // 2
    weights = call(
        prepare_kernel,
        [shape((pairs, 2 * cols, 2 * cols), BF16)] * 2 + [shape((levels, entries * levels), BF16)] * 2,
        (lateral_mix, vertical_mix),
        [VMEM] * 2,
        moved=1 << 21,
    )

    inner = (blocks - 2 * REACH) * cols
    stage = pltpu.VMEM((moments, entries * levels, inner), BF16)
    inner_residual, inner_pulled = call(
        interior_kernel,
        [shape((moments, levels, inner), BF16), shape((moments, levels, inner), F32)],
        (info, neighbours, incr, costate, crossed, *weights),
        [SMEM] * 2 + [VMEM] * 7,
        scratch=[pltpu.VMEM((levels, cols_all), BF16)] * 2 + [stage],
        flops=2_000_000_000,
        moved=4 << 20,
    )

    outer = pltpu.VMEM((moments, entries * levels, 2 * width), BF16)
    residual, adjoint, image = call(
        functools.partial(final_kernel, packed),
        [shape(incr.shape, BF16), shape(incr.shape, BF16), shape((moments, slots), F32)],
        (
            info, neighbours, obs_count, incr, costate, crossed, first, second, arrived, obs_block,
            *weights, inner_residual, inner_pulled,
        ),
        [SMEM] * 3 + [VMEM] * 13,
        scratch=[pltpu.VMEM((moments, levels, cols_all + 2 * width), BF16)] * 2
        + [outer, pltpu.VMEM((moments, levels, 2 * width), F32), pltpu.VMEM((cols_all, slots), BF16)],
        flops=2_000_000_000,
        moved=6 << 20,
    )
    return residual, adjoint, image


def solution(mesh):
    fields = P(("groups", "tm"), None, "space")
    rows = P(("groups", "tm"), "space")
    in_specs = (
        fields, fields, P(), P(), P(("groups", "space"), None), fields, fields, rows, rows, rows,
    )
    return jax.shard_map(
        on_device, mesh=mesh, in_specs=in_specs, out_specs=(fields, fields, rows), check_vma=False
    )
```

```python
import functools

import jax
import jax.numpy as jnp
from jax import lax
from jax.experimental import pallas as pl
from jax.experimental.pallas import tpu as pltpu
from jax.sharding import PartitionSpec as P

REACH = 2
ROW_TILE = 16
FULL = 63.6
BF16 = jnp.bfloat16
F32 = jnp.float32
VMEM = pl.BlockSpec(memory_space=pltpu.VMEM)
ANY = pl.BlockSpec(memory_space=pl.ANY)
HBM = pl.BlockSpec(memory_space=pltpu.HBM)
SMEM = pl.BlockSpec(memory_space=pltpu.SMEM)


def dot(a, b):
    return jnp.dot(a, b, preferred_element_type=F32)


def dot_nt(a, b):
    return lax.dot_general(a, b, (((1,), (1,)), ((), ())), preferred_element_type=F32)


def exchanged(array, pairs):
    both = [(a, b) for a, b in pairs] + [(b, a) for a, b in pairs]
    return lax.ppermute(array, "space", both)


def call(kernel, out_shape, args, specs, out_specs=None, scratch=(), cost=0, limit=16, aliases=None):
    multiple = isinstance(out_shape, (list, tuple))
    return pl.pallas_call(
        kernel,
        out_shape=out_shape,
        in_specs=specs,
        out_specs=out_specs or ([VMEM] * len(out_shape) if multiple else VMEM),
        scratch_shapes=list(scratch),
        input_output_aliases=aliases or {},
        compiler_params=pltpu.CompilerParams(vmem_limit_bytes=int(limit * 1024 * 1024)),
        cost_estimate=pl.CostEstimate(flops=cost * 1_000_000_000, bytes_accessed=cost * 1_000_000, transcendentals=0),
    )(*args)


def gated(data, after):
    return call(gate_kernel, jax.ShapeDtypeStruct(data.shape, BF16), (data, after), [ANY] * 2, ANY, limit=1, aliases={0: 0})


def fetched(pairs, sems):
    copies = [pltpu.make_async_copy(source, target, sems.at[k]) for k, (source, target) in enumerate(pairs)]
    for copy in copies:
        copy.start()
    return copies


def edges_kernel(near_any, incr, costate, crossed, first, second, near, near_sem, sems):
    moments, levels, cols = incr.shape
    blocks, entries = near.shape
    width = first.shape[1]
    place = lax.axis_index("space")
    odd = lax.rem(place, 2)
    fetch = pltpu.make_async_copy(near_any, near, near_sem)
    fetch.start()
    slabs = [incr.at[k] for k in range(moments - 1)] + [costate.at[k] for k in range(1, moments)] + [crossed]
    pairs = []
    for target, right in ((first, 1 - odd), (second, odd)):
        lanes = pl.ds(pl.multiple_of(right * (cols - width), 128), width)
        pairs += [(slab.at[:, lanes], target.at[pl.ds(k * levels, levels)]) for k, slab in enumerate(slabs)]
    copies = fetched(pairs, sems)
    fetch.wait()
    own = lax.broadcasted_iota(jnp.int32, near.shape, 0) + place * blocks
    distance = (near[...] - own).astype(F32)
    distance = jnp.concatenate([distance, jnp.zeros((ROW_TILE - blocks, entries), F32)], axis=0).astype(BF16)
    for target in (first, second):
        target[len(slabs) * levels :] = jnp.zeros((ROW_TILE, width), BF16)
        target[len(slabs) * levels :, :entries] = distance
    for copy in copies:
        copy.wait()


def pack_kernel(lateral_any, vertical_any, weight_any, out, obs_lateral, obs_vertical, obs_weight, sems):
    copies = fetched(
        [(lateral_any, obs_lateral), (vertical_any, obs_vertical), (weight_any, obs_weight)], sems
    )
    for copy in copies:
        copy.wait()
    moments, cols, slots = obs_lateral.shape
    levels = obs_vertical.shape[1]
    tiles = out.shape[0]
    cap = slots // tiles
    for tile in range(tiles):
        lanes = slice(tile * cap, (tile + 1) * cap)
        out[tile, :cols] = jnp.concatenate([obs_lateral[s, :, lanes] for s in range(moments)], axis=1)
        out[tile, cols : cols + levels] = jnp.concatenate(
            [obs_vertical[s, :, lanes] for s in range(moments)], axis=1
        )
        row = jnp.concatenate([obs_weight[s : s + 1, lanes].astype(F32) for s in range(moments)], axis=1)
        out[tile, cols + levels :] = jnp.broadcast_to(row, (ROW_TILE, row.shape[1])).astype(BF16)


def gate_kernel(data, after, out):
    pass


def mixed(get, moments, blocks, entries, pair, vert, stage):
    levels = vert.shape[0]
    cols = pair.shape[1] // 2
    for k in range((entries + 1) // 2):
        single = 2 * k + 1 >= entries
        weight = pair[k, :cols, :cols] if single else pair[k]
        for s in moments:
            rows = []
            for b in blocks:
                part = get(s, b, 2 * k)
                rows.append(part if single else jnp.concatenate([part, get(s, b, 2 * k + 1)], axis=1))
            result = dot(jnp.concatenate(rows, axis=0), weight).astype(BF16)
            for i in range(len(blocks)):
                piece = result[i * levels : (i + 1) * levels]
                lanes = slice(i * cols, (i + 1) * cols)
                stage[s, 2 * k * levels : (2 * k + 1) * levels, lanes] = piece[:, :cols]
                if not single:
                    stage[s, (2 * k + 1) * levels : (2 * k + 2) * levels, lanes] = piece[:, cols:]
    return [(s, dot(vert[...], stage[s])) for s in moments]


def interior_kernel(
    near, counts, incr, costate, crossed, lateral_mix, vertical_mix, owner,
    residual, base, pair_fwd, pair_bwd, vert_fwd, vert_bwd, target, stage,
):
    moments, levels, cols_all = incr.shape
    blocks, entries = near.shape
    cols = cols_all // blocks
    inner = list(range(REACH, blocks - REACH))
    lanes = slice(REACH * cols, (blocks - REACH) * cols)
    tm = lax.axis_index("tm")
    anchor = lax.axis_index("space") * blocks

    pair_fwd[...] = jnp.zeros(pair_fwd.shape, BF16)
    pair_bwd[...] = jnp.zeros(pair_bwd.shape, BF16)
    for j in range(entries):
        at = slice((j % 2) * cols, (j % 2 + 1) * cols)
        pair_fwd[j // 2, at, at] = lateral_mix[j]
        pair_bwd[j // 2, at, at] = lateral_mix[j].astype(F32).T.astype(BF16)
    vert_fwd[...] = jnp.concatenate([vertical_mix[j] for j in range(entries)], axis=1)
    vert_bwd[...] = jnp.concatenate([vertical_mix[j].astype(F32).T.astype(BF16) for j in range(entries)], axis=1)

    tiles = counts.shape[1]
    cap = owner.shape[1] // tiles
    slot = lax.broadcasted_iota(jnp.int32, (1, owner.shape[1]), 1)
    for s in range(moments):
        live = jnp.zeros(slot.shape, jnp.int32)
        for h in range(tiles):
            inside = (slot >= h * cap) & (slot < h * cap + counts[s, h])
            live = jnp.where(inside, 1, live)
        target[s : s + 1] = jnp.where(live == 1, owner[s : s + 1], -1)

    def forward(s, b, j):
        at = pl.ds(pl.multiple_of((near[b, j] - anchor) * cols, cols), cols)
        return crossed[:, at] if s == 0 else incr[s - 1, :, at]

    def backward(s, n, j):
        total = None
        for b in range(n - REACH, n + REACH + 1):
            at = slice(b * cols, (b + 1) * cols)
            source = crossed[:, at] if s == moments - 1 else costate[s + 1, :, at]
            term = jnp.where(near[b, j] == anchor + n, source, jnp.zeros_like(source))
            total = term if total is None else total + term
        return total

    def run_forward(which):
        for s, pushed in mixed(forward, which, inner, entries, pair_fwd, vert_fwd, stage):
            residual[s] = (incr[s, :, lanes].astype(F32) - pushed).astype(BF16)

    def run_backward(which):
        for s, value in mixed(backward, which, inner, entries, pair_bwd, vert_bwd, stage):
            base[s] = costate[s, :, lanes].astype(F32) - value

    @pl.when(tm == 0)
    def _():
        residual[0] = incr[0, :, lanes]
        run_backward([moments - 1])

    @pl.when(tm == 1)
    def _():
        run_forward([0])
        base[moments - 1] = costate[moments - 1, :, lanes].astype(F32)

    run_forward(range(1, moments))
    run_backward(range(moments - 1))


def edge_kernel(
    near, incr, costate, crossed, first, second, pair_fwd, pair_bwd, vert_fwd, vert_bwd, inner_residual,
    residual_any, base, residual, before, after, stage, sems,
):
    moments, levels, cols_all = incr.shape
    blocks, entries = near.shape
    cols = cols_all // blocks
    width = REACH * cols
    place = lax.axis_index("space")
    odd = lax.rem(place, 2)
    tm = lax.axis_index("tm")
    anchor = place * blocks
    outer = [b for b in range(blocks) if b < REACH or b >= blocks - REACH]
    reach_cols = 3 * width

    def fill(target, s, source, edge):
        rows = slice(edge * levels, (edge + 1) * levels)
        one, two = first[rows], second[rows]
        target[s, :, :width] = jnp.where(odd == 1, one, two)
        target[s, :, width:reach_cols] = source[:, : 2 * width]
        target[s, :, reach_cols : reach_cols + 2 * width] = source[:, cols_all - 2 * width :]
        target[s, :, reach_cols + 2 * width :] = jnp.where(odd == 1, two, one)

    for s in range(moments - 1):
        fill(before, s + 1, incr[s], s)
        fill(after, s, costate[s + 1], moments - 1 + s)
    def forward(s, b, j):
        start = REACH if b < REACH else 5 * REACH - blocks
        at = pl.ds(pl.multiple_of((near[b, j] - anchor + start) * cols, cols), cols)
        return before[s, :, at]

    tail = slice((2 * moments - 1) * levels, (2 * moments - 1) * levels + ROW_TILE)
    one, two = first[tail, :cols].astype(F32), second[tail, :cols].astype(F32)
    left = jnp.where(odd == 1, one, two)
    right = jnp.where(odd == 1, two, one)

    def backward(s, n, j):
        total = None
        for b in range(n - REACH, n + REACH + 1):
            start = REACH if n < REACH else 5 * REACH - blocks
            source = after[s, :, (b + start) * cols : (b + start + 1) * cols]
            if 0 <= b < blocks:
                term = jnp.where(near[b, j] == anchor + n, source, jnp.zeros_like(source))
            else:
                row = b + blocks if b < 0 else b - blocks
                offset = (left if b < 0 else right)[row : row + 1, j : j + 1]
                hit = jnp.where(offset == float(n - b), 1.0, 0.0)
                term = source * jnp.broadcast_to(hit, source.shape).astype(BF16)
            total = term if total is None else total + term
        return total

    def ends(field, s):
        return jnp.concatenate([field[s, :, :width], field[s, :, cols_all - width :]], axis=1).astype(F32)

    def run_forward(which):
        for s, pushed in mixed(forward, which, outer, entries, pair_fwd, vert_fwd, stage):
            residual[s, :, :width] = (incr[s, :, :width].astype(F32) - pushed[:, :width]).astype(BF16)
            residual[s, :, width : cols_all - width] = inner_residual[s]
            residual[s, :, cols_all - width :] = (
                incr[s, :, cols_all - width :].astype(F32) - pushed[:, width:]
            ).astype(BF16)

    def run_backward(which):
        for s, value in mixed(backward, which, outer, entries, pair_bwd, vert_bwd, stage):
            base[s] = ends(costate, s) - value

    @pl.when(tm == 0)
    def _():
        residual[0] = incr[0]
        fill(after, moments - 1, crossed[...], 2 * (moments - 1))
        run_backward([moments - 1])

    @pl.when(tm == 1)
    def _():
        fill(before, 0, crossed[...], 2 * (moments - 1))
        run_forward([0])
        base[moments - 1] = ends(costate, moments - 1)

    run_forward(range(1, moments))
    copies = fetched([(residual.at[s], residual_any.at[s]) for s in range(moments)], sems)
    run_backward(range(moments - 1))
    for copy in copies:
        copy.wait()


def observe_kernel(packed, incr, arrived, target, inner_base, outer_base, adjoint_any, image, adjoint, masked, sems):
    moments, levels, cols_all = incr.shape
    slots = target.shape[1]
    width = outer_base.shape[2] // 2
    cols = width // REACH
    blocks = cols_all // cols
    inner_lanes = slice(width, cols_all - width)
    copies = []
    for s in range(moments):
        block = target[s : s + 1]
        if packed:
            cap = arrived.shape[2] // moments
            part = slice(s * cap, (s + 1) * cap)
            whole = jnp.concatenate([arrived[h, :, part] for h in range(arrived.shape[0])], axis=1)
        else:
            whole = arrived[s]
        lateral = whole[:cols]
        vertical = whole[cols : cols + levels].astype(F32)
        weight = whole[cols + levels : cols + levels + ROW_TILE].astype(F32)[:1]
        for b in range(blocks):
            hit = jnp.where(block == b, 1.0, 0.0)
            masked[s % 2, b * cols : (b + 1) * cols] = lateral * jnp.broadcast_to(hit, lateral.shape).astype(BF16)
        along = dot(incr[s], masked[s % 2])
        image[s : s + 1] = jnp.sum(vertical * along, axis=0, keepdims=True)
        push = dot_nt((vertical * weight).astype(BF16), masked[s % 2])
        adjoint[s, :, :width] = (outer_base[s, :, :width] + push[:, :width]).astype(BF16)
        adjoint[s, :, inner_lanes] = (inner_base[s] + push[:, inner_lanes]).astype(BF16)
        adjoint[s, :, cols_all - width :] = (outer_base[s, :, width:] + push[:, cols_all - width :]).astype(BF16)
        copies += fetched([(adjoint.at[s], adjoint_any.at[s])], sems.at[pl.ds(s, 1)])
    for copy in copies:
        copy.wait()


def on_device(
    incr, costate, lateral_mix, vertical_mix, neighbours,
    obs_lateral, obs_vertical, obs_weight, obs_block, obs_count,
):
    moments, levels, cols_all = incr.shape
    entries, cols, _ = lateral_mix.shape
    blocks = neighbours.shape[0]
    slots = obs_block.shape[1]
    tiles = lax.axis_size("space")
    cap = slots // tiles
    width = REACH * cols
    tm = lax.axis_index("tm")
    shape = jax.ShapeDtypeStruct
    semaphores = pltpu.SemaphoreType.DMA

    crossed = lax.ppermute(jnp.where(tm == 0, incr[-1], costate[0]), "tm", [(0, 1), (1, 0)])

    height = cols + levels + ROW_TILE
    packed = moments * cap == 128
    if packed:
        outgoing = call(
            pack_kernel,
            shape((tiles, height, moments * cap), BF16),
            (obs_lateral, obs_vertical, obs_weight),
            [ANY] * 3,
            scratch=[pltpu.VMEM(a.shape, BF16) for a in (obs_lateral, obs_vertical, obs_weight)] + [semaphores((3,))],
            cost=1,
        )
    else:
        stacked = jnp.concatenate(
            [obs_lateral, obs_vertical, jnp.broadcast_to(obs_weight[:, None], (moments, ROW_TILE, slots))], axis=1
        )
        outgoing = stacked.reshape(moments, height, tiles, cap).transpose(2, 1, 0, 3).reshape(tiles, height, -1)

    halo = shape(((2 * moments - 1) * levels + ROW_TILE, width), BF16)
    first, second = call(
        edges_kernel,
        [halo, halo],
        (neighbours, incr, costate, crossed),
        [ANY] * 4,
        scratch=[pltpu.VMEM(neighbours.shape, jnp.int32), semaphores, semaphores((4 * moments - 2,))],
        cost=1,
    )
    outgoing = gated(outgoing, first)
    first = exchanged(first, [(i, i + 1) for i in range(0, tiles - 1, 2)])
    second = exchanged(second, [(i, i + 1) for i in range(1, tiles - 1, 2)])
    arrived = lax.all_to_all(outgoing, "space", split_axis=0, concat_axis=0, tiled=True)
    if not packed:
        arrived = arrived.reshape(tiles, height, moments, cap).transpose(2, 1, 0, 3).reshape(moments, height, slots)

    pairs = (entries + 1) // 2
    inner = cols_all - 2 * width
    inner_residual, inner_base, *weights, target = call(
        interior_kernel,
        [shape((moments, levels, inner), BF16), shape((moments, levels, inner), F32)]
        + [shape((pairs, 2 * cols, 2 * cols), BF16)] * 2
        + [shape((levels, entries * levels), BF16)] * 2
        + [shape(obs_block.shape, jnp.int32)],
        (neighbours, obs_count, incr, costate, crossed, lateral_mix, vertical_mix, obs_block),
        [SMEM] * 2 + [VMEM] * 6,
        scratch=[pltpu.VMEM((moments, entries * levels, inner), BF16)],
        cost=4,
    )

    residual, outer_base = call(
        edge_kernel,
        [shape(incr.shape, BF16), shape((moments, levels, 2 * width), F32)],
        (neighbours, incr, costate, crossed, first, second, *weights, inner_residual),
        [SMEM] + [VMEM] * 10,
        out_specs=[HBM, VMEM],
        scratch=[pltpu.VMEM(incr.shape, BF16)]
        + [pltpu.VMEM((moments, levels, 6 * width), BF16)] * 2
        + [pltpu.VMEM((moments, entries * levels, 2 * width), BF16), semaphores((moments,))],
        cost=4,
    )

    adjoint, image = call(
        functools.partial(observe_kernel, packed),
        [shape(incr.shape, BF16), shape((moments, slots), F32)],
        (incr, arrived, target, inner_base, outer_base),
        [VMEM] * 5,
        out_specs=[HBM, VMEM],
        scratch=[pltpu.VMEM(incr.shape, BF16), pltpu.VMEM((2, cols_all, slots), BF16), semaphores((moments,))],
        cost=3,
    )
    return residual, adjoint, image


def solution(mesh):
    fields = P(("groups", "tm"), None, "space")
    rows = P(("groups", "tm"), "space")
    in_specs = (
        fields, fields, P(), P(), P(("groups", "space"), None), fields, fields, rows, rows, rows,
    )
    return jax.shard_map(
        on_device, mesh=mesh, in_specs=in_specs, out_specs=(fields, fields, rows), check_vma=False
    )
```

```python
import functools

import jax
import jax.numpy as jnp
from jax import lax
from jax.experimental import pallas as pl
from jax.experimental.pallas import tpu as pltpu
from jax.sharding import PartitionSpec as P

REACH = 2
ROWS = 8
FULL = 63.6
BF16 = jnp.bfloat16
F32 = jnp.float32
VMEM = pl.BlockSpec(memory_space=pltpu.VMEM)
ANY = pl.BlockSpec(memory_space=pl.ANY)
HBM = pl.BlockSpec(memory_space=pltpu.HBM)
SMEM = pl.BlockSpec(memory_space=pltpu.SMEM)


def dot(a, b):
    return jnp.dot(a, b, preferred_element_type=F32)


def dot_nt(a, b):
    return lax.dot_general(a, b, (((1,), (1,)), ((), ())), preferred_element_type=F32)


def exchanged(array, pairs):
    both = [(a, b) for a, b in pairs] + [(b, a) for a, b in pairs]
    return lax.ppermute(array, "space", both)


def call(kernel, out_shape, args, specs, out_specs=None, scratch=(), cost=0, limit=16, aliases=None):
    multiple = isinstance(out_shape, (list, tuple))
    return pl.pallas_call(
        kernel,
        out_shape=out_shape,
        in_specs=specs,
        out_specs=out_specs or ([VMEM] * len(out_shape) if multiple else VMEM),
        scratch_shapes=list(scratch),
        input_output_aliases=aliases or {},
        compiler_params=pltpu.CompilerParams(vmem_limit_bytes=int(limit * 1024 * 1024)),
        cost_estimate=pl.CostEstimate(flops=cost * 1_000_000_000, bytes_accessed=cost * 1_000_000, transcendentals=0),
    )(*args)


def gated(data, after):
    return call(gate_kernel, jax.ShapeDtypeStruct(data.shape, BF16), (data, after), [ANY] * 2, ANY, limit=1, aliases={0: 0})


def fetched(pairs, sems):
    copies = [pltpu.make_async_copy(source, target, sems.at[k]) for k, (source, target) in enumerate(pairs)]
    for copy in copies:
        copy.start()
    return copies


def edges_kernel(near_any, incr, costate, crossed, first, second, near, near_sem, sems):
    moments, levels, cols = incr.shape
    blocks, entries = near.shape
    width = first.shape[1]
    place = lax.axis_index("space")
    odd = lax.rem(place, 2)
    fetch = pltpu.make_async_copy(near_any, near, near_sem)
    fetch.start()
    slabs = [incr.at[k] for k in range(moments - 1)] + [costate.at[k] for k in range(1, moments)] + [crossed]
    pairs = []
    for target, right in ((first, 1 - odd), (second, odd)):
        lanes = pl.ds(pl.multiple_of(right * (cols - width), 128), width)
        pairs += [(slab.at[:, lanes], target.at[pl.ds(k * levels, levels)]) for k, slab in enumerate(slabs)]
    copies = fetched(pairs, sems)
    fetch.wait()
    own = lax.broadcasted_iota(jnp.int32, near.shape, 0) + place * blocks
    distance = (near[...] - own).astype(F32)
    distance = distance.astype(BF16)
    for target in (first, second):
        target[len(slabs) * levels :] = jnp.zeros((ROWS, width), BF16)
        target[len(slabs) * levels :, :entries] = distance
    for copy in copies:
        copy.wait()


def pack_kernel(lateral_any, vertical_any, weight_any, out, obs_lateral, obs_vertical, obs_weight, sems):
    copies = fetched(
        [(lateral_any, obs_lateral), (vertical_any, obs_vertical), (weight_any, obs_weight)], sems
    )
    for copy in copies:
        copy.wait()
    moments, cols, slots = obs_lateral.shape
    levels = obs_vertical.shape[1]
    tiles = out.shape[0]
    cap = slots // tiles
    for tile in range(tiles):
        lanes = slice(tile * cap, (tile + 1) * cap)
        out[tile, :cols] = jnp.concatenate([obs_lateral[s, :, lanes] for s in range(moments)], axis=1)
        out[tile, cols : cols + levels] = jnp.concatenate(
            [obs_vertical[s, :, lanes] for s in range(moments)], axis=1
        )
        row = jnp.concatenate([obs_weight[s : s + 1, lanes].astype(F32) for s in range(moments)], axis=1)
        out[tile, cols + levels :] = jnp.broadcast_to(row, (ROWS, row.shape[1])).astype(BF16)


def gate_kernel(data, after, out):
    pass


def mixed(get, moments, blocks, entries, pair, vert, stage):
    levels = vert.shape[0]
    cols = pair.shape[1] // 2
    for k in range((entries + 1) // 2):
        single = 2 * k + 1 >= entries
        weight = pair[k, :cols, :cols] if single else pair[k]
        for s in moments:
            rows = []
            for b in blocks:
                part = get(s, b, 2 * k)
                rows.append(part if single else jnp.concatenate([part, get(s, b, 2 * k + 1)], axis=1))
            result = dot(jnp.concatenate(rows, axis=0), weight).astype(BF16)
            for i in range(len(blocks)):
                piece = result[i * levels : (i + 1) * levels]
                lanes = slice(i * cols, (i + 1) * cols)
                stage[s, 2 * k * levels : (2 * k + 1) * levels, lanes] = piece[:, :cols]
                if not single:
                    stage[s, (2 * k + 1) * levels : (2 * k + 2) * levels, lanes] = piece[:, cols:]
    return [(s, dot(vert[...], stage[s])) for s in moments]


def interior_kernel(
    near, counts, incr, costate, crossed, lateral_mix, vertical_mix, owner,
    residual, base, pair_fwd, pair_bwd, vert_fwd, vert_bwd, target, stage,
):
    moments, levels, cols_all = incr.shape
    blocks, entries = near.shape
    cols = cols_all // blocks
    inner = list(range(REACH, blocks - REACH))
    lanes = slice(REACH * cols, (blocks - REACH) * cols)
    tm = lax.axis_index("tm")
    anchor = lax.axis_index("space") * blocks

    pair_fwd[...] = jnp.zeros(pair_fwd.shape, BF16)
    pair_bwd[...] = jnp.zeros(pair_bwd.shape, BF16)
    for j in range(entries):
        at = slice((j % 2) * cols, (j % 2 + 1) * cols)
        pair_fwd[j // 2, at, at] = lateral_mix[j]
        pair_bwd[j // 2, at, at] = lateral_mix[j].astype(F32).T.astype(BF16)
    vert_fwd[...] = jnp.concatenate([vertical_mix[j] for j in range(entries)], axis=1)
    vert_bwd[...] = jnp.concatenate([vertical_mix[j].astype(F32).T.astype(BF16) for j in range(entries)], axis=1)

    tiles = counts.shape[1]
    cap = owner.shape[1] // tiles
    slot = lax.broadcasted_iota(jnp.int32, (1, owner.shape[1]), 1)
    for s in range(moments):
        live = jnp.zeros(slot.shape, jnp.int32)
        for h in range(tiles):
            inside = (slot >= h * cap) & (slot < h * cap + counts[s, h])
            live = jnp.where(inside, 1, live)
        target[s : s + 1] = jnp.where(live == 1, owner[s : s + 1], -1)

    def forward(s, b, j):
        at = pl.ds(pl.multiple_of((near[b, j] - anchor) * cols, cols), cols)
        return crossed[:, at] if s == 0 else incr[s - 1, :, at]

    def backward(s, n, j):
        total = None
        for b in range(n - REACH, n + REACH + 1):
            at = slice(b * cols, (b + 1) * cols)
            source = crossed[:, at] if s == moments - 1 else costate[s + 1, :, at]
            term = jnp.where(near[b, j] == anchor + n, source, jnp.zeros_like(source))
            total = term if total is None else total + term
        return total

    def run_forward(which):
        for s, pushed in mixed(forward, which, inner, entries, pair_fwd, vert_fwd, stage):
            residual[s] = (incr[s, :, lanes].astype(F32) - pushed).astype(BF16)

    def run_backward(which):
        for s, value in mixed(backward, which, inner, entries, pair_bwd, vert_bwd, stage):
            base[s] = costate[s, :, lanes].astype(F32) - value

    @pl.when(tm == 0)
    def _():
        residual[0] = incr[0, :, lanes]
        run_backward([moments - 1])

    @pl.when(tm == 1)
    def _():
        run_forward([0])
        base[moments - 1] = costate[moments - 1, :, lanes].astype(F32)

    run_forward(range(1, moments))
    run_backward(range(moments - 1))


def edge_kernel(
    near, incr, costate, crossed, first, second, pair_fwd, pair_bwd, vert_fwd, vert_bwd, inner_residual,
    residual_any, *rest,
):
    moments, levels, cols_all = incr.shape
    base = rest[:moments]
    residual, before, after, stage, sems = rest[moments:]
    blocks, entries = near.shape
    cols = cols_all // blocks
    width = REACH * cols
    place = lax.axis_index("space")
    odd = lax.rem(place, 2)
    tm = lax.axis_index("tm")
    anchor = place * blocks
    outer = [b for b in range(blocks) if b < REACH or b >= blocks - REACH]
    reach_cols = 3 * width

    def fill(target, s, source, edge):
        rows = slice(edge * levels, (edge + 1) * levels)
        one, two = first[rows], second[rows]
        target[s, :, :width] = jnp.where(odd == 1, one, two)
        target[s, :, width:reach_cols] = source[:, : 2 * width]
        target[s, :, reach_cols : reach_cols + 2 * width] = source[:, cols_all - 2 * width :]
        target[s, :, reach_cols + 2 * width :] = jnp.where(odd == 1, two, one)

    for s in range(moments - 1):
        fill(before, s + 1, incr[s], s)
        fill(after, s, costate[s + 1], moments - 1 + s)
    def forward(s, b, j):
        start = REACH if b < REACH else 5 * REACH - blocks
        at = pl.ds(pl.multiple_of((near[b, j] - anchor + start) * cols, cols), cols)
        return before[s, :, at]

    tail = slice((2 * moments - 1) * levels, (2 * moments - 1) * levels + ROWS)
    one, two = first[tail, :cols].astype(F32), second[tail, :cols].astype(F32)
    left = jnp.where(odd == 1, one, two)
    right = jnp.where(odd == 1, two, one)

    def backward(s, n, j):
        total = None
        for b in range(n - REACH, n + REACH + 1):
            start = REACH if n < REACH else 5 * REACH - blocks
            source = after[s, :, (b + start) * cols : (b + start + 1) * cols]
            if 0 <= b < blocks:
                term = jnp.where(near[b, j] == anchor + n, source, jnp.zeros_like(source))
            else:
                row = b + blocks if b < 0 else b - blocks
                offset = (left if b < 0 else right)[row : row + 1, j : j + 1]
                hit = jnp.where(offset == float(n - b), 1.0, 0.0)
                term = source * jnp.broadcast_to(hit, source.shape).astype(BF16)
            total = term if total is None else total + term
        return total

    def ends(field, s):
        return jnp.concatenate([field[s, :, :width], field[s, :, cols_all - width :]], axis=1).astype(F32)

    def run_forward(which):
        for s, pushed in mixed(forward, which, outer, entries, pair_fwd, vert_fwd, stage):
            residual[s, :, :width] = (incr[s, :, :width].astype(F32) - pushed[:, :width]).astype(BF16)
            residual[s, :, width : cols_all - width] = inner_residual[s]
            residual[s, :, cols_all - width :] = (
                incr[s, :, cols_all - width :].astype(F32) - pushed[:, width:]
            ).astype(BF16)

    def run_backward(which):
        for s, value in mixed(backward, which, outer, entries, pair_bwd, vert_bwd, stage):
            base[s][...] = ends(costate, s) - value

    @pl.when(tm == 0)
    def _():
        residual[0] = incr[0]
        fill(after, moments - 1, crossed[...], 2 * (moments - 1))
        run_backward([moments - 1])

    @pl.when(tm == 1)
    def _():
        fill(before, 0, crossed[...], 2 * (moments - 1))
        run_forward([0])
        base[moments - 1][...] = ends(costate, moments - 1)

    run_forward(range(1, moments))
    copies = fetched([(residual.at[s], residual_any.at[s]) for s in range(moments)], sems)
    run_backward(range(moments - 1))
    for copy in copies:
        copy.wait()


def observe_kernel(packed, incr, arrived, target, inner_base, *rest):
    moments, levels, cols_all = incr.shape
    outer_base = rest[:moments]
    adjoint_any, image, adjoint, masked, sems = rest[moments:]
    slots = target.shape[1]
    width = outer_base[0].shape[1] // 2
    cols = width // REACH
    blocks = cols_all // cols
    inner_lanes = slice(width, cols_all - width)
    copies = []
    for s in range(moments):
        block = target[s : s + 1]
        if packed:
            cap = arrived.shape[2] // moments
            part = slice(s * cap, (s + 1) * cap)
            whole = jnp.concatenate([arrived[h, :, part] for h in range(arrived.shape[0])], axis=1)
        else:
            whole = arrived[s]
        lateral = whole[:cols]
        vertical = whole[cols : cols + levels].astype(F32)
        weight = whole[cols + levels : cols + levels + ROWS].astype(F32)[:1]
        for b in range(blocks):
            hit = jnp.where(block == b, 1.0, 0.0)
            masked[s % 2, b * cols : (b + 1) * cols] = lateral * jnp.broadcast_to(hit, lateral.shape).astype(BF16)
        along = dot(incr[s], masked[s % 2])
        image[s : s + 1] = jnp.sum(vertical * along, axis=0, keepdims=True)
        push = dot_nt((vertical * weight).astype(BF16), masked[s % 2])
        adjoint[s, :, :width] = (outer_base[s][:, :width] + push[:, :width]).astype(BF16)
        adjoint[s, :, inner_lanes] = (inner_base[s] + push[:, inner_lanes]).astype(BF16)
        adjoint[s, :, cols_all - width :] = (outer_base[s][:, width:] + push[:, cols_all - width :]).astype(BF16)
        copies += fetched([(adjoint.at[s], adjoint_any.at[s])], sems.at[pl.ds(s, 1)])
    for copy in copies:
        copy.wait()


def on_device(
    incr, costate, lateral_mix, vertical_mix, neighbours,
    obs_lateral, obs_vertical, obs_weight, obs_block, obs_count,
):
    moments, levels, cols_all = incr.shape
    entries, cols, _ = lateral_mix.shape
    blocks = neighbours.shape[0]
    slots = obs_block.shape[1]
    tiles = lax.axis_size("space")
    cap = slots // tiles
    width = REACH * cols
    tm = lax.axis_index("tm")
    shape = jax.ShapeDtypeStruct
    semaphores = pltpu.SemaphoreType.DMA

    crossed = lax.ppermute(jnp.where(tm == 0, incr[-1], costate[0]), "tm", [(0, 1), (1, 0)])

    height = cols + levels + ROWS
    packed = moments * cap == 128
    if packed:
        outgoing = call(
            pack_kernel,
            shape((tiles, height, moments * cap), BF16),
            (obs_lateral, obs_vertical, obs_weight),
            [ANY] * 3,
            scratch=[pltpu.VMEM(a.shape, BF16) for a in (obs_lateral, obs_vertical, obs_weight)] + [semaphores((3,))],
            cost=1,
        )
    else:
        stacked = jnp.concatenate(
            [obs_lateral, obs_vertical, jnp.broadcast_to(obs_weight[:, None], (moments, ROWS, slots))], axis=1
        )
        outgoing = stacked.reshape(moments, height, tiles, cap).transpose(2, 1, 0, 3).reshape(tiles, height, -1)

    halo = shape(((2 * moments - 1) * levels + ROWS, width), BF16)
    first, second = call(
        edges_kernel,
        [halo, halo],
        (neighbours, incr, costate, crossed),
        [ANY] * 4,
        scratch=[pltpu.VMEM(neighbours.shape, jnp.int32), semaphores, semaphores((4 * moments - 2,))],
        cost=1,
    )
    outgoing = gated(outgoing, first)
    first = exchanged(first, [(i, i + 1) for i in range(0, tiles - 1, 2)])
    second = exchanged(second, [(i, i + 1) for i in range(1, tiles - 1, 2)])
    arrived = lax.all_to_all(outgoing, "space", split_axis=0, concat_axis=0, tiled=True)
    if not packed:
        arrived = arrived.reshape(tiles, height, moments, cap).transpose(2, 1, 0, 3).reshape(moments, height, slots)

    pairs = (entries + 1) // 2
    inner = cols_all - 2 * width
    inner_residual, inner_base, *weights, target = call(
        interior_kernel,
        [shape((moments, levels, inner), BF16), shape((moments, levels, inner), F32)]
        + [shape((pairs, 2 * cols, 2 * cols), BF16)] * 2
        + [shape((levels, entries * levels), BF16)] * 2
        + [shape(obs_block.shape, jnp.int32)],
        (neighbours, obs_count, incr, costate, crossed, lateral_mix, vertical_mix, obs_block),
        [SMEM] * 2 + [VMEM] * 6,
        scratch=[pltpu.VMEM((moments, entries * levels, inner), BF16)],
        cost=4,
    )

    residual, *outer_base = call(
        edge_kernel,
        [shape(incr.shape, BF16)] + [shape((levels, 2 * width), F32)] * moments,
        (neighbours, incr, costate, crossed, first, second, *weights, inner_residual),
        [SMEM] + [VMEM] * 10,
        out_specs=[HBM] + [VMEM] * moments,
        scratch=[pltpu.VMEM(incr.shape, BF16)]
        + [pltpu.VMEM((moments, levels, 6 * width), BF16)] * 2
        + [pltpu.VMEM((moments, entries * levels, 2 * width), BF16), semaphores((moments,))],
        cost=4,
    )

    adjoint, image = call(
        functools.partial(observe_kernel, packed),
        [shape(incr.shape, BF16), shape((moments, slots), F32)],
        (incr, arrived, target, inner_base, *outer_base),
        [VMEM] * (4 + moments),
        out_specs=[HBM, VMEM],
        scratch=[pltpu.VMEM(incr.shape, BF16), pltpu.VMEM((2, cols_all, slots), BF16), semaphores((moments,))],
        cost=3,
    )
    return residual, adjoint, image


def solution(mesh):
    fields = P(("groups", "tm"), None, "space")
    rows = P(("groups", "tm"), "space")
    in_specs = (
        fields, fields, P(), P(), P(("groups", "space"), None), fields, fields, rows, rows, rows,
    )
    return jax.shard_map(
        on_device, mesh=mesh, in_specs=in_specs, out_specs=(fields, fields, rows), check_vma=False
    )
```

```python
import functools

import jax
import jax.numpy as jnp
from jax import lax
from jax.experimental import pallas as pl
from jax.experimental.pallas import tpu as pltpu
from jax.sharding import PartitionSpec as P

REACH = 2
ROWS = 8
FULL = 63.6
BF16 = jnp.bfloat16
F32 = jnp.float32
VMEM = pl.BlockSpec(memory_space=pltpu.VMEM)
ANY = pl.BlockSpec(memory_space=pl.ANY)
HBM = pl.BlockSpec(memory_space=pltpu.HBM)
SMEM = pl.BlockSpec(memory_space=pltpu.SMEM)


def dot(a, b):
    return jnp.dot(a, b, preferred_element_type=F32)


def dot_nt(a, b):
    return lax.dot_general(a, b, (((1,), (1,)), ((), ())), preferred_element_type=F32)


def exchanged(array, pairs):
    both = [(a, b) for a, b in pairs] + [(b, a) for a, b in pairs]
    return lax.ppermute(array, "space", both)


def call(kernel, out_shape, args, specs, out_specs=None, scratch=(), cost=0, limit=16, aliases=None):
    multiple = isinstance(out_shape, (list, tuple))
    return pl.pallas_call(
        kernel,
        out_shape=out_shape,
        in_specs=specs,
        out_specs=out_specs or ([VMEM] * len(out_shape) if multiple else VMEM),
        scratch_shapes=list(scratch),
        input_output_aliases=aliases or {},
        compiler_params=pltpu.CompilerParams(vmem_limit_bytes=int(limit * 1024 * 1024)),
        cost_estimate=pl.CostEstimate(flops=cost * 1_000_000_000, bytes_accessed=cost * 1_000_000, transcendentals=0),
    )(*args)


def gated(data, after):
    return call(gate_kernel, jax.ShapeDtypeStruct(data.shape, BF16), (data, after), [ANY] * 2, ANY, limit=1, aliases={0: 0})


def fetched(pairs, sems):
    copies = [pltpu.make_async_copy(source, target, sems.at[k]) for k, (source, target) in enumerate(pairs)]
    for copy in copies:
        copy.start()
    return copies


def edges_kernel(near_any, incr, costate, crossed, first, second, near, near_sem, sems):
    moments, levels, cols = incr.shape
    blocks, entries = near.shape
    width = first.shape[1]
    place = lax.axis_index("space")
    odd = lax.rem(place, 2)
    fetch = pltpu.make_async_copy(near_any, near, near_sem)
    fetch.start()
    slabs = [incr.at[k] for k in range(moments - 1)] + [costate.at[k] for k in range(1, moments)] + [crossed]
    pairs = []
    for target, right in ((first, 1 - odd), (second, odd)):
        lanes = pl.ds(pl.multiple_of(right * (cols - width), 128), width)
        pairs += [(slab.at[:, lanes], target.at[pl.ds(k * levels, levels)]) for k, slab in enumerate(slabs)]
    copies = fetched(pairs, sems)
    fetch.wait()
    own = lax.broadcasted_iota(jnp.int32, near.shape, 0) + place * blocks
    distance = (near[...] - own).astype(F32)
    distance = distance.astype(BF16)
    for target in (first, second):
        target[len(slabs) * levels :] = jnp.zeros((ROWS, width), BF16)
        target[len(slabs) * levels :, :entries] = distance
    for copy in copies:
        copy.wait()


def pack_kernel(lateral_any, vertical_any, weight_any, out_any, out, obs_lateral, obs_vertical, obs_weight, sems, out_sems):
    copies = fetched(
        [(lateral_any, obs_lateral), (vertical_any, obs_vertical), (weight_any, obs_weight)], sems
    )
    for copy in copies:
        copy.wait()
    moments, cols, slots = obs_lateral.shape
    copies = []
    levels = obs_vertical.shape[1]
    tiles = out.shape[0]
    cap = slots // tiles
    for tile in range(tiles):
        lanes = slice(tile * cap, (tile + 1) * cap)
        out[tile, :cols] = jnp.concatenate([obs_lateral[s, :, lanes] for s in range(moments)], axis=1)
        out[tile, cols : cols + levels] = jnp.concatenate(
            [obs_vertical[s, :, lanes] for s in range(moments)], axis=1
        )
        row = jnp.concatenate([obs_weight[s : s + 1, lanes].astype(F32) for s in range(moments)], axis=1)
        out[tile, cols + levels :] = jnp.broadcast_to(row, (ROWS, row.shape[1])).astype(BF16)
        copies += fetched([(out.at[tile], out_any.at[tile])], out_sems.at[pl.ds(tile, 1)])
    for copy in copies:
        copy.wait()


def gate_kernel(data, after, out):
    pass


def mixed(get, moments, blocks, entries, pair, vert, stage):
    levels = vert.shape[0]
    cols = pair.shape[1] // 2
    for k in range((entries + 1) // 2):
        single = 2 * k + 1 >= entries
        weight = pair[k, :cols, :cols] if single else pair[k]
        rows = []
        for s in moments:
            for b in blocks:
                part = get(s, b, 2 * k)
                rows.append(part if single else jnp.concatenate([part, get(s, b, 2 * k + 1)], axis=1))
        result = dot(jnp.concatenate(rows, axis=0), weight).astype(BF16)
        for i, (s, n) in enumerate((s, n) for s in moments for n in range(len(blocks))):
            piece = result[i * levels : (i + 1) * levels]
            lanes = slice(n * cols, (n + 1) * cols)
            stage[s, 2 * k * levels : (2 * k + 1) * levels, lanes] = piece[:, :cols]
            if not single:
                stage[s, (2 * k + 1) * levels : (2 * k + 2) * levels, lanes] = piece[:, cols:]
    return [(s, dot(vert[...], stage[s])) for s in moments]


def interior_kernel(
    near, counts, incr, costate, crossed, lateral_mix, vertical_mix, owner,
    residual, base, pair_fwd, pair_bwd, vert_fwd, vert_bwd, target, stage,
):
    moments, levels, cols_all = incr.shape
    blocks, entries = near.shape
    cols = cols_all // blocks
    inner = list(range(REACH, blocks - REACH))
    lanes = slice(REACH * cols, (blocks - REACH) * cols)
    tm = lax.axis_index("tm")
    anchor = lax.axis_index("space") * blocks

    pair_fwd[...] = jnp.zeros(pair_fwd.shape, BF16)
    pair_bwd[...] = jnp.zeros(pair_bwd.shape, BF16)
    for j in range(entries):
        at = slice((j % 2) * cols, (j % 2 + 1) * cols)
        pair_fwd[j // 2, at, at] = lateral_mix[j]
        pair_bwd[j // 2, at, at] = lateral_mix[j].astype(F32).T.astype(BF16)
    vert_fwd[...] = jnp.concatenate([vertical_mix[j] for j in range(entries)], axis=1)
    vert_bwd[...] = jnp.concatenate([vertical_mix[j].astype(F32).T.astype(BF16) for j in range(entries)], axis=1)

    tiles = counts.shape[1]
    cap = owner.shape[1] // tiles
    slot = lax.broadcasted_iota(jnp.int32, (1, owner.shape[1]), 1)
    for s in range(moments):
        live = jnp.zeros(slot.shape, jnp.int32)
        for h in range(tiles):
            inside = (slot >= h * cap) & (slot < h * cap + counts[s, h])
            live = jnp.where(inside, 1, live)
        target[s : s + 1] = jnp.where(live == 1, owner[s : s + 1], -1)

    def forward(s, b, j):
        at = pl.ds(pl.multiple_of((near[b, j] - anchor) * cols, cols), cols)
        return crossed[:, at] if s == 0 else incr[s - 1, :, at]

    def backward(s, n, j):
        total = None
        for b in range(n - REACH, n + REACH + 1):
            at = slice(b * cols, (b + 1) * cols)
            source = crossed[:, at] if s == moments - 1 else costate[s + 1, :, at]
            term = jnp.where(near[b, j] == anchor + n, source, jnp.zeros_like(source))
            total = term if total is None else total + term
        return total

    def run_forward(which):
        for s, pushed in mixed(forward, which, inner, entries, pair_fwd, vert_fwd, stage):
            residual[s] = (incr[s, :, lanes].astype(F32) - pushed).astype(BF16)

    def run_backward(which):
        for s, value in mixed(backward, which, inner, entries, pair_bwd, vert_bwd, stage):
            base[s] = costate[s, :, lanes].astype(F32) - value

    @pl.when(tm == 0)
    def _():
        residual[0] = incr[0, :, lanes]
        run_backward([moments - 1])

    @pl.when(tm == 1)
    def _():
        run_forward([0])
        base[moments - 1] = costate[moments - 1, :, lanes].astype(F32)

    run_forward(range(1, moments))
    run_backward(range(moments - 1))


def edge_kernel(
    near, incr, costate, crossed, first, second, pair_fwd, pair_bwd, vert_fwd, vert_bwd, inner_residual,
    residual_any, *rest,
):
    moments, levels, cols_all = incr.shape
    base = rest[:moments]
    residual, before, after, stage, sems = rest[moments:]
    blocks, entries = near.shape
    cols = cols_all // blocks
    width = REACH * cols
    place = lax.axis_index("space")
    odd = lax.rem(place, 2)
    tm = lax.axis_index("tm")
    anchor = place * blocks
    outer = [b for b in range(blocks) if b < REACH or b >= blocks - REACH]
    reach_cols = 3 * width

    def fill(target, s, source, edge):
        rows = slice(edge * levels, (edge + 1) * levels)
        one, two = first[rows], second[rows]
        target[s, :, :width] = jnp.where(odd == 1, one, two)
        target[s, :, width:reach_cols] = source[:, : 2 * width]
        target[s, :, reach_cols : reach_cols + 2 * width] = source[:, cols_all - 2 * width :]
        target[s, :, reach_cols + 2 * width :] = jnp.where(odd == 1, two, one)

    for s in range(moments - 1):
        fill(before, s + 1, incr[s], s)
        fill(after, s, costate[s + 1], moments - 1 + s)
    def forward(s, b, j):
        start = REACH if b < REACH else 5 * REACH - blocks
        at = pl.ds(pl.multiple_of((near[b, j] - anchor + start) * cols, cols), cols)
        return before[s, :, at]

    tail = slice((2 * moments - 1) * levels, (2 * moments - 1) * levels + ROWS)
    one, two = first[tail, :cols].astype(F32), second[tail, :cols].astype(F32)
    left = jnp.where(odd == 1, one, two)
    right = jnp.where(odd == 1, two, one)

    def backward(s, n, j):
        total = None
        for b in range(n - REACH, n + REACH + 1):
            start = REACH if n < REACH else 5 * REACH - blocks
            source = after[s, :, (b + start) * cols : (b + start + 1) * cols]
            if 0 <= b < blocks:
                term = jnp.where(near[b, j] == anchor + n, source, jnp.zeros_like(source))
            else:
                row = b + blocks if b < 0 else b - blocks
                offset = (left if b < 0 else right)[row : row + 1, j : j + 1]
                hit = jnp.where(offset == float(n - b), 1.0, 0.0)
                term = source * jnp.broadcast_to(hit, source.shape).astype(BF16)
            total = term if total is None else total + term
        return total

    def ends(field, s):
        return jnp.concatenate([field[s, :, :width], field[s, :, cols_all - width :]], axis=1).astype(F32)

    def run_forward(which):
        for s, pushed in mixed(forward, which, outer, entries, pair_fwd, vert_fwd, stage):
            residual[s, :, :width] = (incr[s, :, :width].astype(F32) - pushed[:, :width]).astype(BF16)
            residual[s, :, width : cols_all - width] = inner_residual[s]
            residual[s, :, cols_all - width :] = (
                incr[s, :, cols_all - width :].astype(F32) - pushed[:, width:]
            ).astype(BF16)

    def run_backward(which):
        for s, value in mixed(backward, which, outer, entries, pair_bwd, vert_bwd, stage):
            base[s][...] = ends(costate, s) - value

    @pl.when(tm == 0)
    def _():
        residual[0] = incr[0]
        fill(after, moments - 1, crossed[...], 2 * (moments - 1))
        run_backward([moments - 1])

    @pl.when(tm == 1)
    def _():
        fill(before, 0, crossed[...], 2 * (moments - 1))
        run_forward([0])
        base[moments - 1][...] = ends(costate, moments - 1)

    run_forward(range(1, moments))
    copies = fetched([(residual.at[s], residual_any.at[s]) for s in range(moments)], sems)
    run_backward(range(moments - 1))
    for copy in copies:
        copy.wait()


def observe_kernel(packed, incr, arrived, target, inner_base, *rest):
    moments, levels, cols_all = incr.shape
    outer_base = rest[:moments]
    adjoint_any, image_any, adjoint, image, sems = rest[moments:]
    slots = target.shape[1]
    width = outer_base[0].shape[1] // 2
    cols = width // REACH
    blocks = cols_all // cols
    inner_lanes = slice(width, cols_all - width)
    copies = []
    for s in range(moments):
        block = target[s : s + 1]
        if packed:
            cap = arrived.shape[2] // moments
            part = slice(s * cap, (s + 1) * cap)
            whole = jnp.concatenate([arrived[h, :, part] for h in range(arrived.shape[0])], axis=1)
        else:
            whole = arrived[s]
        lateral = whole[:cols]
        vertical = whole[cols : cols + levels].astype(F32)
        weight = whole[cols + levels :].astype(F32)[:1]
        hits = [jnp.where(block == b, 1.0, 0.0) for b in range(blocks)]
        fields = jnp.concatenate([incr[s, :, b * cols : (b + 1) * cols] for b in range(blocks)], axis=0)
        seen = dot(fields, lateral)
        along = sum(hits[b] * seen[b * levels : (b + 1) * levels] for b in range(blocks))
        image[s : s + 1] = jnp.sum(vertical * along, axis=0, keepdims=True)
        if s == moments - 1:
            copies += fetched([(image, image_any)], sems.at[pl.ds(moments, 1)])
        scaled = (vertical * weight).astype(BF16)
        parts = [scaled * jnp.broadcast_to(hit, scaled.shape).astype(BF16) for hit in hits]
        stacked = dot_nt(jnp.concatenate(parts, axis=0), lateral)
        push = jnp.concatenate([stacked[b * levels : (b + 1) * levels] for b in range(blocks)], axis=1)
        adjoint[s, :, :width] = (outer_base[s][:, :width] + push[:, :width]).astype(BF16)
        adjoint[s, :, inner_lanes] = (inner_base[s] + push[:, inner_lanes]).astype(BF16)
        adjoint[s, :, cols_all - width :] = (outer_base[s][:, width:] + push[:, cols_all - width :]).astype(BF16)
        copies += fetched([(adjoint.at[s], adjoint_any.at[s])], sems.at[pl.ds(s, 1)])
    for copy in copies:
        copy.wait()


def on_device(
    incr, costate, lateral_mix, vertical_mix, neighbours,
    obs_lateral, obs_vertical, obs_weight, obs_block, obs_count,
):
    moments, levels, cols_all = incr.shape
    entries, cols, _ = lateral_mix.shape
    blocks = neighbours.shape[0]
    slots = obs_block.shape[1]
    tiles = lax.axis_size("space")
    cap = slots // tiles
    width = REACH * cols
    tm = lax.axis_index("tm")
    shape = jax.ShapeDtypeStruct
    semaphores = pltpu.SemaphoreType.DMA

    crossed = lax.ppermute(jnp.where(tm == 0, incr[-1], costate[0]), "tm", [(0, 1), (1, 0)])

    height = cols + levels + ROWS
    packed = moments * cap == 128
    if packed:
        outgoing = call(
            pack_kernel,
            shape((tiles, height, moments * cap), BF16),
            (obs_lateral, obs_vertical, obs_weight),
            [ANY] * 3,
            out_specs=HBM,
            scratch=[pltpu.VMEM((tiles, height, moments * cap), BF16)]
            + [pltpu.VMEM(a.shape, BF16) for a in (obs_lateral, obs_vertical, obs_weight)]
            + [semaphores((3,)), semaphores((tiles,))],
            cost=1,
        )
    else:
        stacked = jnp.concatenate(
            [obs_lateral, obs_vertical, jnp.broadcast_to(obs_weight[:, None], (moments, ROWS, slots))], axis=1
        )
        outgoing = stacked.reshape(moments, height, tiles, cap).transpose(2, 1, 0, 3).reshape(tiles, height, -1)

    halo = shape(((2 * moments - 1) * levels + ROWS, width), BF16)
    first, second = call(
        edges_kernel,
        [halo, halo],
        (neighbours, incr, costate, crossed),
        [ANY] * 4,
        scratch=[pltpu.VMEM(neighbours.shape, jnp.int32), semaphores, semaphores((4 * moments - 2,))],
        cost=1,
    )
    outgoing = gated(outgoing, first)
    first = exchanged(first, [(i, i + 1) for i in range(0, tiles - 1, 2)])
    second = exchanged(second, [(i, i + 1) for i in range(1, tiles - 1, 2)])
    arrived = lax.all_to_all(outgoing, "space", split_axis=0, concat_axis=0, tiled=True)
    if not packed:
        arrived = arrived.reshape(tiles, height, moments, cap).transpose(2, 1, 0, 3).reshape(moments, height, slots)

    pairs = (entries + 1) // 2
    inner = cols_all - 2 * width
    inner_residual, inner_base, *weights, target = call(
        interior_kernel,
        [shape((moments, levels, inner), BF16), shape((moments, levels, inner), F32)]
        + [shape((pairs, 2 * cols, 2 * cols), BF16)] * 2
        + [shape((levels, entries * levels), BF16)] * 2
        + [shape(obs_block.shape, jnp.int32)],
        (neighbours, obs_count, incr, costate, crossed, lateral_mix, vertical_mix, obs_block),
        [SMEM] * 2 + [VMEM] * 6,
        scratch=[pltpu.VMEM((moments, entries * levels, inner), BF16)],
        cost=4,
    )

    residual, *outer_base = call(
        edge_kernel,
        [shape(incr.shape, BF16)] + [shape((levels, 2 * width), F32)] * moments,
        (neighbours, incr, costate, crossed, first, second, *weights, inner_residual),
        [SMEM] + [VMEM] * 10,
        out_specs=[HBM] + [VMEM] * moments,
        scratch=[pltpu.VMEM(incr.shape, BF16)]
        + [pltpu.VMEM((moments, levels, 6 * width), BF16)] * 2
        + [pltpu.VMEM((moments, entries * levels, 2 * width), BF16), semaphores((moments,))],
        cost=4,
    )

    adjoint, image = call(
        functools.partial(observe_kernel, packed),
        [shape(incr.shape, BF16), shape((moments, slots), F32)],
        (incr, arrived, target, inner_base, *outer_base),
        [VMEM] * (4 + moments),
        out_specs=[HBM, HBM],
        scratch=[pltpu.VMEM(incr.shape, BF16), pltpu.VMEM((moments, slots), F32), semaphores((moments + 1,))],
        cost=3,
    )
    return residual, adjoint, image


def solution(mesh):
    fields = P(("groups", "tm"), None, "space")
    rows = P(("groups", "tm"), "space")
    in_specs = (
        fields, fields, P(), P(), P(("groups", "space"), None), fields, fields, rows, rows, rows,
    )
    return jax.shard_map(
        on_device, mesh=mesh, in_specs=in_specs, out_specs=(fields, fields, rows), check_vma=False
    )
```

```python
import functools

import jax
import jax.numpy as jnp
from jax import lax
from jax.experimental import pallas as pl
from jax.experimental.pallas import tpu as pltpu
from jax.sharding import PartitionSpec as P

REACH = 2
ROWS = 8
FULL = 63.6
BF16 = jnp.bfloat16
F32 = jnp.float32
VMEM = pl.BlockSpec(memory_space=pltpu.VMEM)
ANY = pl.BlockSpec(memory_space=pl.ANY)
HBM = pl.BlockSpec(memory_space=pltpu.HBM)
SMEM = pl.BlockSpec(memory_space=pltpu.SMEM)


def dot(a, b):
    return jnp.dot(a, b, preferred_element_type=F32)


def dot_nt(a, b):
    return lax.dot_general(a, b, (((1,), (1,)), ((), ())), preferred_element_type=F32)


def exchanged(array, pairs):
    both = [(a, b) for a, b in pairs] + [(b, a) for a, b in pairs]
    return lax.ppermute(array, "space", both)


def call(kernel, out_shape, args, specs, out_specs=None, scratch=(), cost=0, limit=16, aliases=None):
    multiple = isinstance(out_shape, (list, tuple))
    return pl.pallas_call(
        kernel,
        out_shape=out_shape,
        in_specs=specs,
        out_specs=out_specs or ([VMEM] * len(out_shape) if multiple else VMEM),
        scratch_shapes=list(scratch),
        input_output_aliases=aliases or {},
        compiler_params=pltpu.CompilerParams(vmem_limit_bytes=int(limit * 1024 * 1024)),
        cost_estimate=pl.CostEstimate(flops=cost * 1_000_000_000, bytes_accessed=cost * 1_000_000, transcendentals=0),
    )(*args)


def gated(data, after):
    return call(gate_kernel, jax.ShapeDtypeStruct(data.shape, BF16), (data, after), [ANY] * 2, ANY, limit=1, aliases={0: 0})


def fetched(pairs, sems):
    copies = [pltpu.make_async_copy(source, target, sems.at[k]) for k, (source, target) in enumerate(pairs)]
    for copy in copies:
        copy.start()
    return copies


def edges_kernel(near_any, incr, costate, crossed, first, second, near, near_sem, sems):
    moments, levels, cols = incr.shape
    blocks, entries = near.shape
    width = first.shape[1]
    place = lax.axis_index("space")
    odd = lax.rem(place, 2)
    fetch = pltpu.make_async_copy(near_any, near, near_sem)
    fetch.start()
    slabs = [incr.at[k] for k in range(moments - 1)] + [costate.at[k] for k in range(1, moments)] + [crossed]
    pairs = []
    for target, right in ((first, 1 - odd), (second, odd)):
        lanes = pl.ds(pl.multiple_of(right * (cols - width), 128), width)
        pairs += [(slab.at[:, lanes], target.at[pl.ds(k * levels, levels)]) for k, slab in enumerate(slabs)]
    copies = fetched(pairs, sems)
    fetch.wait()
    own = lax.broadcasted_iota(jnp.int32, near.shape, 0) + place * blocks
    distance = (near[...] - own).astype(F32)
    distance = distance.astype(BF16)
    for target in (first, second):
        target[len(slabs) * levels :] = jnp.zeros((ROWS, width), BF16)
        target[len(slabs) * levels :, :entries] = distance
    for copy in copies:
        copy.wait()


def pack_kernel(obs_lateral, obs_vertical, obs_weight, out_any, out, out_sems):
    moments, cols, slots = obs_lateral.shape
    copies = []
    levels = obs_vertical.shape[1]
    tiles = out.shape[0]
    cap = slots // tiles
    for tile in range(tiles):
        lanes = slice(tile * cap, (tile + 1) * cap)
        out[tile, :cols] = jnp.concatenate([obs_lateral[s, :, lanes] for s in range(moments)], axis=1)
        out[tile, cols : cols + levels] = jnp.concatenate(
            [obs_vertical[s, :, lanes] for s in range(moments)], axis=1
        )
        row = jnp.concatenate([obs_weight[s : s + 1, lanes].astype(F32) for s in range(moments)], axis=1)
        out[tile, cols + levels :] = jnp.broadcast_to(row, (ROWS, row.shape[1])).astype(BF16)
        copies += fetched([(out.at[tile], out_any.at[tile])], out_sems.at[pl.ds(tile, 1)])
    for copy in copies:
        copy.wait()


def gate_kernel(data, after, out):
    pass


def mixed(get, moments, blocks, entries, pair, vert, stage):
    levels = vert.shape[0]
    cols = pair.shape[1] // 2
    for k in range((entries + 1) // 2):
        single = 2 * k + 1 >= entries
        weight = pair[k, :cols, :cols] if single else pair[k]
        rows = []
        for s in moments:
            for b in blocks:
                part = get(s, b, 2 * k)
                rows.append(part if single else jnp.concatenate([part, get(s, b, 2 * k + 1)], axis=1))
        result = dot(jnp.concatenate(rows, axis=0), weight).astype(BF16)
        for i, (s, n) in enumerate((s, n) for s in moments for n in range(len(blocks))):
            piece = result[i * levels : (i + 1) * levels]
            lanes = slice(n * cols, (n + 1) * cols)
            stage[s, 2 * k * levels : (2 * k + 1) * levels, lanes] = piece[:, :cols]
            if not single:
                stage[s, (2 * k + 1) * levels : (2 * k + 2) * levels, lanes] = piece[:, cols:]
    return [(s, dot(vert[...], stage[s])) for s in moments]


def interior_kernel(
    near, counts, incr, costate, crossed, lateral_mix, vertical_mix, owner,
    residual, base, pair_fwd, pair_bwd, vert_fwd, vert_bwd, target, stage,
):
    moments, levels, cols_all = incr.shape
    blocks, entries = near.shape
    cols = cols_all // blocks
    inner = list(range(REACH, blocks - REACH))
    lanes = slice(REACH * cols, (blocks - REACH) * cols)
    tm = lax.axis_index("tm")
    anchor = lax.axis_index("space") * blocks

    pair_fwd[...] = jnp.zeros(pair_fwd.shape, BF16)
    pair_bwd[...] = jnp.zeros(pair_bwd.shape, BF16)
    for j in range(entries):
        at = slice((j % 2) * cols, (j % 2 + 1) * cols)
        pair_fwd[j // 2, at, at] = lateral_mix[j]
        pair_bwd[j // 2, at, at] = lateral_mix[j].astype(F32).T.astype(BF16)
    vert_fwd[...] = jnp.concatenate([vertical_mix[j] for j in range(entries)], axis=1)
    vert_bwd[...] = jnp.concatenate([vertical_mix[j].astype(F32).T.astype(BF16) for j in range(entries)], axis=1)

    tiles = counts.shape[1]
    cap = owner.shape[1] // tiles
    slot = lax.broadcasted_iota(jnp.int32, (1, owner.shape[1]), 1)
    for s in range(moments):
        live = jnp.zeros(slot.shape, jnp.int32)
        for h in range(tiles):
            inside = (slot >= h * cap) & (slot < h * cap + counts[s, h])
            live = jnp.where(inside, 1, live)
        target[s : s + 1] = jnp.where(live == 1, owner[s : s + 1], -1)

    def forward(s, b, j):
        at = pl.ds(pl.multiple_of((near[b, j] - anchor) * cols, cols), cols)
        return crossed[:, at] if s == 0 else incr[s - 1, :, at]

    def backward(s, n, j):
        total = None
        for b in range(n - REACH, n + REACH + 1):
            at = slice(b * cols, (b + 1) * cols)
            source = crossed[:, at] if s == moments - 1 else costate[s + 1, :, at]
            term = jnp.where(near[b, j] == anchor + n, source, jnp.zeros_like(source)).astype(F32)
            total = term if total is None else total + term
        return total.astype(BF16)

    def run_forward(which):
        for s, pushed in mixed(forward, which, inner, entries, pair_fwd, vert_fwd, stage):
            residual[s] = (incr[s, :, lanes].astype(F32) - pushed).astype(BF16)

    def run_backward(which):
        for s, value in mixed(backward, which, inner, entries, pair_bwd, vert_bwd, stage):
            base[s] = costate[s, :, lanes].astype(F32) - value

    @pl.when(tm == 0)
    def _():
        residual[0] = incr[0, :, lanes]
        run_backward([moments - 1])

    @pl.when(tm == 1)
    def _():
        run_forward([0])
        base[moments - 1] = costate[moments - 1, :, lanes].astype(F32)

    run_forward(range(1, moments))
    run_backward(range(moments - 1))


def edge_kernel(
    near, incr, costate, crossed, first, second, pair_fwd, pair_bwd, vert_fwd, vert_bwd, inner_residual,
    residual_any, *rest,
):
    moments, levels, cols_all = incr.shape
    base = rest[:moments]
    residual, before, after, stage, sems = rest[moments:]
    blocks, entries = near.shape
    cols = cols_all // blocks
    width = REACH * cols
    place = lax.axis_index("space")
    odd = lax.rem(place, 2)
    tm = lax.axis_index("tm")
    anchor = place * blocks
    outer = [b for b in range(blocks) if b < REACH or b >= blocks - REACH]
    reach_cols = 3 * width

    def fill(target, s, source, edge):
        rows = slice(edge * levels, (edge + 1) * levels)
        one, two = first[rows], second[rows]
        target[s, :, :width] = jnp.where(odd == 1, one, two)
        target[s, :, width:reach_cols] = source[:, : 2 * width]
        target[s, :, reach_cols : reach_cols + 2 * width] = source[:, cols_all - 2 * width :]
        target[s, :, reach_cols + 2 * width :] = jnp.where(odd == 1, two, one)

    for s in range(moments - 1):
        fill(before, s + 1, incr[s], s)
        fill(after, s, costate[s + 1], moments - 1 + s)
    def forward(s, b, j):
        start = REACH if b < REACH else 5 * REACH - blocks
        at = pl.ds(pl.multiple_of((near[b, j] - anchor + start) * cols, cols), cols)
        return before[s, :, at]

    tail = slice((2 * moments - 1) * levels, (2 * moments - 1) * levels + ROWS)
    one, two = first[tail, :cols].astype(F32), second[tail, :cols].astype(F32)
    left = jnp.where(odd == 1, one, two)
    right = jnp.where(odd == 1, two, one)

    def backward(s, n, j):
        total = None
        for b in range(n - REACH, n + REACH + 1):
            start = REACH if n < REACH else 5 * REACH - blocks
            source = after[s, :, (b + start) * cols : (b + start + 1) * cols]
            if 0 <= b < blocks:
                term = jnp.where(near[b, j] == anchor + n, source, jnp.zeros_like(source))
            else:
                row = b + blocks if b < 0 else b - blocks
                offset = (left if b < 0 else right)[row : row + 1, j : j + 1]
                hit = jnp.where(offset == float(n - b), 1.0, 0.0)
                term = source * jnp.broadcast_to(hit, source.shape).astype(BF16)
            total = term.astype(F32) if total is None else total + term.astype(F32)
        return total.astype(BF16)

    def ends(field, s):
        return jnp.concatenate([field[s, :, :width], field[s, :, cols_all - width :]], axis=1).astype(F32)

    def run_forward(which):
        for s, pushed in mixed(forward, which, outer, entries, pair_fwd, vert_fwd, stage):
            residual[s, :, :width] = (incr[s, :, :width].astype(F32) - pushed[:, :width]).astype(BF16)
            residual[s, :, width : cols_all - width] = inner_residual[s]
            residual[s, :, cols_all - width :] = (
                incr[s, :, cols_all - width :].astype(F32) - pushed[:, width:]
            ).astype(BF16)

    def run_backward(which):
        for s, value in mixed(backward, which, outer, entries, pair_bwd, vert_bwd, stage):
            base[s][...] = ends(costate, s) - value

    @pl.when(tm == 0)
    def _():
        residual[0] = incr[0]
        fill(after, moments - 1, crossed[...], 2 * (moments - 1))
        run_backward([moments - 1])

    @pl.when(tm == 1)
    def _():
        fill(before, 0, crossed[...], 2 * (moments - 1))
        run_forward([0])
        base[moments - 1][...] = ends(costate, moments - 1)

    run_forward(range(1, moments))
    copies = fetched([(residual.at[s], residual_any.at[s]) for s in range(moments)], sems)
    run_backward(range(moments - 1))
    for copy in copies:
        copy.wait()


def observe_kernel(packed, incr, arrived, target, inner_base, *rest):
    moments, levels, cols_all = incr.shape
    outer_base = rest[:moments]
    adjoint_any, image_any, adjoint, image, sems = rest[moments:]
    slots = target.shape[1]
    width = outer_base[0].shape[1] // 2
    cols = width // REACH
    blocks = cols_all // cols
    inner_lanes = slice(width, cols_all - width)
    copies = []
    for s in range(moments):
        block = target[s : s + 1]
        if packed:
            cap = arrived.shape[2] // moments
            part = slice(s * cap, (s + 1) * cap)
            whole = jnp.concatenate([arrived[h, :, part] for h in range(arrived.shape[0])], axis=1)
        else:
            whole = arrived[s]
        lateral = whole[:cols]
        vertical = whole[cols : cols + levels].astype(F32)
        weight = whole[cols + levels :].astype(F32)[:1]
        hits = [jnp.where(block == b, 1.0, 0.0) for b in range(blocks)]
        fields = jnp.concatenate([incr[s, :, b * cols : (b + 1) * cols] for b in range(blocks)], axis=0)
        seen = dot(fields, lateral)
        along = sum(hits[b] * seen[b * levels : (b + 1) * levels] for b in range(blocks))
        image[s : s + 1] = jnp.sum(vertical * along, axis=0, keepdims=True)
        if s == moments - 1:
            copies += fetched([(image, image_any)], sems.at[pl.ds(moments, 1)])
        scaled = (vertical * weight).astype(BF16)
        parts = [scaled * jnp.broadcast_to(hit, scaled.shape).astype(BF16) for hit in hits]
        stacked = dot_nt(jnp.concatenate(parts, axis=0), lateral)
        push = jnp.concatenate([stacked[b * levels : (b + 1) * levels] for b in range(blocks)], axis=1)
        adjoint[s, :, :width] = (outer_base[s][:, :width] + push[:, :width]).astype(BF16)
        adjoint[s, :, inner_lanes] = (inner_base[s] + push[:, inner_lanes]).astype(BF16)
        adjoint[s, :, cols_all - width :] = (outer_base[s][:, width:] + push[:, cols_all - width :]).astype(BF16)
        copies += fetched([(adjoint.at[s], adjoint_any.at[s])], sems.at[pl.ds(s, 1)])
    for copy in copies:
        copy.wait()


def on_device(
    incr, costate, lateral_mix, vertical_mix, neighbours,
    obs_lateral, obs_vertical, obs_weight, obs_block, obs_count,
):
    moments, levels, cols_all = incr.shape
    entries, cols, _ = lateral_mix.shape
    blocks = neighbours.shape[0]
    slots = obs_block.shape[1]
    tiles = lax.axis_size("space")
    cap = slots // tiles
    width = REACH * cols
    tm = lax.axis_index("tm")
    shape = jax.ShapeDtypeStruct
    semaphores = pltpu.SemaphoreType.DMA

    crossed = lax.ppermute(jnp.where(tm == 0, incr[-1], costate[0]), "tm", [(0, 1), (1, 0)])

    height = cols + levels + ROWS
    packed = moments * cap == 128
    if packed:
        outgoing = call(
            pack_kernel,
            shape((tiles, height, moments * cap), BF16),
            (obs_lateral, obs_vertical, obs_weight),
            [VMEM] * 3,
            out_specs=HBM,
            scratch=[pltpu.VMEM((tiles, height, moments * cap), BF16), semaphores((tiles,))],
            cost=1,
        )
    else:
        stacked = jnp.concatenate(
            [obs_lateral, obs_vertical, jnp.broadcast_to(obs_weight[:, None], (moments, ROWS, slots))], axis=1
        )
        outgoing = stacked.reshape(moments, height, tiles, cap).transpose(2, 1, 0, 3).reshape(tiles, height, -1)

    halo = shape(((2 * moments - 1) * levels + ROWS, width), BF16)
    first, second = call(
        edges_kernel,
        [halo, halo],
        (neighbours, incr, costate, crossed),
        [ANY] * 4,
        scratch=[pltpu.VMEM(neighbours.shape, jnp.int32), semaphores, semaphores((4 * moments - 2,))],
        cost=1,
    )
    outgoing = gated(outgoing, first)
    first = exchanged(first, [(i, i + 1) for i in range(0, tiles - 1, 2)])
    second = exchanged(second, [(i, i + 1) for i in range(1, tiles - 1, 2)])
    arrived = lax.all_to_all(outgoing, "space", split_axis=0, concat_axis=0, tiled=True)
    if not packed:
        arrived = arrived.reshape(tiles, height, moments, cap).transpose(2, 1, 0, 3).reshape(moments, height, slots)

    pairs = (entries + 1) // 2
    inner = cols_all - 2 * width
    inner_residual, inner_base, *weights, target = call(
        interior_kernel,
        [shape((moments, levels, inner), BF16), shape((moments, levels, inner), F32)]
        + [shape((pairs, 2 * cols, 2 * cols), BF16)] * 2
        + [shape((levels, entries * levels), BF16)] * 2
        + [shape(obs_block.shape, jnp.int32)],
        (neighbours, obs_count, incr, costate, crossed, lateral_mix, vertical_mix, obs_block),
        [SMEM] * 2 + [VMEM] * 6,
        scratch=[pltpu.VMEM((moments, entries * levels, inner), BF16)],
        cost=4,
    )

    residual, *outer_base = call(
        edge_kernel,
        [shape(incr.shape, BF16)] + [shape((levels, 2 * width), F32)] * moments,
        (neighbours, incr, costate, crossed, first, second, *weights, inner_residual),
        [SMEM] + [VMEM] * 10,
        out_specs=[HBM] + [VMEM] * moments,
        scratch=[pltpu.VMEM(incr.shape, BF16)]
        + [pltpu.VMEM((moments, levels, 6 * width), BF16)] * 2
        + [pltpu.VMEM((moments, entries * levels, 2 * width), BF16), semaphores((moments,))],
        cost=4,
    )

    adjoint, image = call(
        functools.partial(observe_kernel, packed),
        [shape(incr.shape, BF16), shape((moments, slots), F32)],
        (incr, arrived, target, inner_base, *outer_base),
        [VMEM] * (4 + moments),
        out_specs=[HBM, HBM],
        scratch=[pltpu.VMEM(incr.shape, BF16), pltpu.VMEM((moments, slots), F32), semaphores((moments + 1,))],
        cost=3,
    )
    return residual, adjoint, image


def solution(mesh):
    fields = P(("groups", "tm"), None, "space")
    rows = P(("groups", "tm"), "space")
    in_specs = (
        fields, fields, P(), P(), P(("groups", "space"), None), fields, fields, rows, rows, rows,
    )
    return jax.shard_map(
        on_device, mesh=mesh, in_specs=in_specs, out_specs=(fields, fields, rows), check_vma=False
    )
```

```python
import functools

import jax
import jax.numpy as jnp
from jax import lax
from jax.experimental import pallas as pl
from jax.experimental.pallas import tpu as pltpu
from jax.sharding import PartitionSpec as P

REACH = 2
ROWS = 16
BF16 = jnp.bfloat16
F32 = jnp.float32
VMEM = pl.BlockSpec(memory_space=pltpu.VMEM)
ANY = pl.BlockSpec(memory_space=pl.ANY)
HBM = pl.BlockSpec(memory_space=pltpu.HBM)
SMEM = pl.BlockSpec(memory_space=pltpu.SMEM)


def dot(a, b):
    return jnp.dot(a, b, preferred_element_type=F32)


def dot_nt(a, b):
    return lax.dot_general(a, b, (((1,), (1,)), ((), ())), preferred_element_type=F32)


def exchanged(array, pairs):
    both = [(a, b) for a, b in pairs] + [(b, a) for a, b in pairs]
    return lax.ppermute(array, "space", both)


def call(kernel, out_shape, args, specs, out_specs=None, scratch=(), cost=0, limit=16, aliases=None):
    multiple = isinstance(out_shape, (list, tuple))
    return pl.pallas_call(
        kernel,
        out_shape=out_shape,
        in_specs=specs,
        out_specs=out_specs or ([VMEM] * len(out_shape) if multiple else VMEM),
        scratch_shapes=list(scratch),
        input_output_aliases=aliases or {},
        compiler_params=pltpu.CompilerParams(vmem_limit_bytes=limit * 1024 * 1024),
        cost_estimate=pl.CostEstimate(flops=cost * 1_000_000_000, bytes_accessed=cost * 1_000_000, transcendentals=0),
    )(*args)


def gated(data, after):
    return call(gate_kernel, jax.ShapeDtypeStruct(data.shape, BF16), (data, after), [ANY] * 2, ANY, limit=1, aliases={0: 0})


def fetched(pairs, sems):
    copies = [pltpu.make_async_copy(source, target, sems.at[k]) for k, (source, target) in enumerate(pairs)]
    for copy in copies:
        copy.start()
    return copies


def edges_kernel(near_any, incr, costate, crossed, first, second, near, near_sem, sems):
    moments, levels, cols = incr.shape
    blocks, entries = near.shape
    width = first.shape[1]
    place = lax.axis_index("space")
    odd = lax.rem(place, 2)
    fetch = pltpu.make_async_copy(near_any, near, near_sem)
    fetch.start()
    slabs = [incr.at[k] for k in range(moments - 1)] + [costate.at[k] for k in range(1, moments)] + [crossed]
    pairs = []
    for target, right in ((first, 1 - odd), (second, odd)):
        lanes = pl.ds(pl.multiple_of(right * (cols - width), 128), width)
        pairs += [(slab.at[:, lanes], target.at[pl.ds(k * levels, levels)]) for k, slab in enumerate(slabs)]
    copies = fetched(pairs, sems)
    fetch.wait()
    own = lax.broadcasted_iota(jnp.int32, near.shape, 0) + place * blocks
    distance = (near[...] - own).astype(F32)
    distance = jnp.concatenate([distance, jnp.zeros((ROWS - blocks, entries), F32)], axis=0).astype(BF16)
    for target in (first, second):
        target[len(slabs) * levels :] = jnp.zeros((ROWS, width), BF16)
        target[len(slabs) * levels :, :entries] = distance
    for copy in copies:
        copy.wait()


def pack_kernel(obs_lateral, obs_vertical, obs_weight, out_any, out, out_sems):
    moments, cols, slots = obs_lateral.shape
    copies = []
    levels = obs_vertical.shape[1]
    tiles = out.shape[0]
    cap = slots // tiles
    for tile in range(tiles):
        lanes = slice(tile * cap, (tile + 1) * cap)
        out[tile, :cols] = jnp.concatenate([obs_lateral[s, :, lanes] for s in range(moments)], axis=1)
        out[tile, cols : cols + levels] = jnp.concatenate(
            [obs_vertical[s, :, lanes] for s in range(moments)], axis=1
        )
        row = jnp.concatenate([obs_weight[s : s + 1, lanes].astype(F32) for s in range(moments)], axis=1)
        out[tile, cols + levels :] = jnp.broadcast_to(row, (ROWS, row.shape[1])).astype(BF16)
        copies += fetched([(out.at[tile], out_any.at[tile])], out_sems.at[pl.ds(tile, 1)])
    for copy in copies:
        copy.wait()


def gate_kernel(data, after, out):
    pass


def mixed(get, moments, blocks, entries, pair, vert, stage):
    levels = vert.shape[0]
    cols = pair.shape[1] // 2
    for k in range((entries + 1) // 2):
        single = 2 * k + 1 >= entries
        weight = pair[k, :cols, :cols] if single else pair[k]
        rows = []
        for s in moments:
            for b in blocks:
                part = get(s, b, 2 * k)
                rows.append(part if single else jnp.concatenate([part, get(s, b, 2 * k + 1)], axis=1))
        result = dot(jnp.concatenate(rows, axis=0), weight).astype(BF16)
        for i, (s, n) in enumerate((s, n) for s in moments for n in range(len(blocks))):
            piece = result[i * levels : (i + 1) * levels]
            lanes = slice(n * cols, (n + 1) * cols)
            stage[s, 2 * k * levels : (2 * k + 1) * levels, lanes] = piece[:, :cols]
            if not single:
                stage[s, (2 * k + 1) * levels : (2 * k + 2) * levels, lanes] = piece[:, cols:]
    return [(s, dot(vert[...], stage[s])) for s in moments]


def interior_kernel(
    near, counts, incr, costate, crossed, lateral_mix, vertical_mix, owner,
    residual, base, pair_fwd, pair_bwd, vert_fwd, vert_bwd, target, stage,
):
    moments, levels, cols_all = incr.shape
    blocks, entries = near.shape
    cols = cols_all // blocks
    inner = list(range(REACH, blocks - REACH))
    lanes = slice(REACH * cols, (blocks - REACH) * cols)
    tm = lax.axis_index("tm")
    anchor = lax.axis_index("space") * blocks

    pair_fwd[...] = jnp.zeros(pair_fwd.shape, BF16)
    pair_bwd[...] = jnp.zeros(pair_bwd.shape, BF16)
    for j in range(entries):
        at = slice((j % 2) * cols, (j % 2 + 1) * cols)
        pair_fwd[j // 2, at, at] = lateral_mix[j]
        pair_bwd[j // 2, at, at] = lateral_mix[j].astype(F32).T.astype(BF16)
    vert_fwd[...] = jnp.concatenate([vertical_mix[j] for j in range(entries)], axis=1)
    vert_bwd[...] = jnp.concatenate([vertical_mix[j].astype(F32).T.astype(BF16) for j in range(entries)], axis=1)

    tiles = counts.shape[1]
    cap = owner.shape[1] // tiles
    slot = lax.broadcasted_iota(jnp.int32, (1, owner.shape[1]), 1)
    for s in range(moments):
        live = jnp.zeros(slot.shape, jnp.int32)
        for h in range(tiles):
            inside = (slot >= h * cap) & (slot < h * cap + counts[s, h])
            live = jnp.where(inside, 1, live)
        target[s : s + 1] = jnp.where(live == 1, owner[s : s + 1], -1)

    def forward(s, b, j):
        at = pl.ds(pl.multiple_of((near[b, j] - anchor) * cols, cols), cols)
        return crossed[:, at] if s == 0 else incr[s - 1, :, at]

    def backward(s, n, j):
        total = None
        for b in range(n - REACH, n + REACH + 1):
            at = slice(b * cols, (b + 1) * cols)
            source = crossed[:, at] if s == moments - 1 else costate[s + 1, :, at]
            term = jnp.where(near[b, j] == anchor + n, source, jnp.zeros_like(source)).astype(F32)
            total = term if total is None else total + term
        return total.astype(BF16)

    def run_forward(which):
        for s, pushed in mixed(forward, which, inner, entries, pair_fwd, vert_fwd, stage):
            residual[s] = (incr[s, :, lanes].astype(F32) - pushed).astype(BF16)

    def run_backward(which):
        for s, value in mixed(backward, which, inner, entries, pair_bwd, vert_bwd, stage):
            base[s] = costate[s, :, lanes].astype(F32) - value

    @pl.when(tm == 0)
    def _():
        residual[0] = incr[0, :, lanes]
        run_backward([moments - 1])

    @pl.when(tm == 1)
    def _():
        run_forward([0])
        base[moments - 1] = costate[moments - 1, :, lanes].astype(F32)

    run_forward(range(1, moments))
    run_backward(range(moments - 1))


def edge_kernel(
    near, incr, costate, crossed, first, second, pair_fwd, pair_bwd, vert_fwd, vert_bwd, inner_residual,
    residual_any, *rest,
):
    moments, levels, cols_all = incr.shape
    base = rest[:moments]
    residual, before, after, stage, sems = rest[moments:]
    blocks, entries = near.shape
    cols = cols_all // blocks
    width = REACH * cols
    place = lax.axis_index("space")
    odd = lax.rem(place, 2)
    tm = lax.axis_index("tm")
    anchor = place * blocks
    outer = [b for b in range(blocks) if b < REACH or b >= blocks - REACH]
    reach_cols = 3 * width

    def fill(target, s, source, edge):
        rows = slice(edge * levels, (edge + 1) * levels)
        one, two = first[rows], second[rows]
        target[s, :, :width] = jnp.where(odd == 1, one, two)
        target[s, :, width:reach_cols] = source[:, : 2 * width]
        target[s, :, reach_cols : reach_cols + 2 * width] = source[:, cols_all - 2 * width :]
        target[s, :, reach_cols + 2 * width :] = jnp.where(odd == 1, two, one)

    for s in range(moments - 1):
        fill(before, s + 1, incr[s], s)
        fill(after, s, costate[s + 1], moments - 1 + s)
    def forward(s, b, j):
        start = REACH if b < REACH else 5 * REACH - blocks
        at = pl.ds(pl.multiple_of((near[b, j] - anchor + start) * cols, cols), cols)
        return before[s, :, at]

    tail = slice((2 * moments - 1) * levels, (2 * moments - 1) * levels + ROWS)
    one, two = first[tail, :cols].astype(F32), second[tail, :cols].astype(F32)
    left = jnp.where(odd == 1, one, two)
    right = jnp.where(odd == 1, two, one)

    def backward(s, n, j):
        total = None
        for b in range(n - REACH, n + REACH + 1):
            start = REACH if n < REACH else 5 * REACH - blocks
            source = after[s, :, (b + start) * cols : (b + start + 1) * cols]
            if 0 <= b < blocks:
                term = jnp.where(near[b, j] == anchor + n, source, jnp.zeros_like(source))
            else:
                row = b + blocks if b < 0 else b - blocks
                offset = (left if b < 0 else right)[row : row + 1, j : j + 1]
                hit = jnp.where(offset == float(n - b), 1.0, 0.0)
                term = source * jnp.broadcast_to(hit, source.shape).astype(BF16)
            total = term.astype(F32) if total is None else total + term.astype(F32)
        return total.astype(BF16)

    def ends(field, s):
        return jnp.concatenate([field[s, :, :width], field[s, :, cols_all - width :]], axis=1).astype(F32)

    def run_forward(which):
        for s, pushed in mixed(forward, which, outer, entries, pair_fwd, vert_fwd, stage):
            residual[s, :, :width] = (incr[s, :, :width].astype(F32) - pushed[:, :width]).astype(BF16)
            residual[s, :, width : cols_all - width] = inner_residual[s]
            residual[s, :, cols_all - width :] = (
                incr[s, :, cols_all - width :].astype(F32) - pushed[:, width:]
            ).astype(BF16)

    def run_backward(which):
        for s, value in mixed(backward, which, outer, entries, pair_bwd, vert_bwd, stage):
            base[s][...] = ends(costate, s) - value

    @pl.when(tm == 0)
    def _():
        residual[0] = incr[0]
        fill(after, moments - 1, crossed[...], 2 * (moments - 1))
        run_backward([moments - 1])

    @pl.when(tm == 1)
    def _():
        fill(before, 0, crossed[...], 2 * (moments - 1))
        run_forward([0])
        base[moments - 1][...] = ends(costate, moments - 1)

    run_forward(range(1, moments))
    copies = fetched([(residual.at[s], residual_any.at[s]) for s in range(moments)], sems)
    run_backward(range(moments - 1))
    for copy in copies:
        copy.wait()


def observe_kernel(packed, incr, arrived, target, inner_base, *rest):
    moments, levels, cols_all = incr.shape
    outer_base = rest[:moments]
    adjoint_any, image_any, adjoint, image, sems = rest[moments:]
    slots = target.shape[1]
    width = outer_base[0].shape[1] // 2
    cols = width // REACH
    blocks = cols_all // cols
    inner_lanes = slice(width, cols_all - width)
    copies = []
    for s in range(moments):
        block = target[s : s + 1]
        if packed:
            cap = arrived.shape[2] // moments
            part = slice(s * cap, (s + 1) * cap)
            whole = jnp.concatenate([arrived[h, :, part] for h in range(arrived.shape[0])], axis=1)
        else:
            whole = arrived[s]
        lateral = whole[:cols]
        vertical = whole[cols : cols + levels].astype(F32)
        weight = whole[cols + levels :].astype(F32)[:1]
        hits = [jnp.where(block == b, 1.0, 0.0) for b in range(blocks)]
        fields = jnp.concatenate([incr[s, :, b * cols : (b + 1) * cols] for b in range(blocks)], axis=0)
        seen = dot(fields, lateral)
        along = sum(hits[b] * seen[b * levels : (b + 1) * levels] for b in range(blocks))
        image[s : s + 1] = jnp.sum(vertical * along, axis=0, keepdims=True)
        if s == moments - 1:
            copies += fetched([(image, image_any)], sems.at[pl.ds(moments, 1)])
        scaled = (vertical * weight).astype(BF16)
        parts = [scaled * jnp.broadcast_to(hit, scaled.shape).astype(BF16) for hit in hits]
        stacked = dot_nt(jnp.concatenate(parts, axis=0), lateral)
        push = jnp.concatenate([stacked[b * levels : (b + 1) * levels] for b in range(blocks)], axis=1)
        adjoint[s, :, :width] = (outer_base[s][:, :width] + push[:, :width]).astype(BF16)
        adjoint[s, :, inner_lanes] = (inner_base[s] + push[:, inner_lanes]).astype(BF16)
        adjoint[s, :, cols_all - width :] = (outer_base[s][:, width:] + push[:, cols_all - width :]).astype(BF16)
        copies += fetched([(adjoint.at[s], adjoint_any.at[s])], sems.at[pl.ds(s, 1)])
    for copy in copies:
        copy.wait()


def on_device(
    incr, costate, lateral_mix, vertical_mix, neighbours,
    obs_lateral, obs_vertical, obs_weight, obs_block, obs_count,
):
    moments, levels, cols_all = incr.shape
    entries, cols, _ = lateral_mix.shape
    blocks = neighbours.shape[0]
    slots = obs_block.shape[1]
    tiles = lax.axis_size("space")
    cap = slots // tiles
    width = REACH * cols
    tm = lax.axis_index("tm")
    shape = jax.ShapeDtypeStruct
    semaphores = pltpu.SemaphoreType.DMA

    crossed = lax.ppermute(jnp.where(tm == 0, incr[-1], costate[0]), "tm", [(0, 1), (1, 0)])

    height = cols + levels + ROWS
    packed = moments * cap == 128
    if packed:
        outgoing = call(
            pack_kernel,
            shape((tiles, height, moments * cap), BF16),
            (obs_lateral, obs_vertical, obs_weight),
            [VMEM] * 3,
            out_specs=HBM,
            scratch=[pltpu.VMEM((tiles, height, moments * cap), BF16), semaphores((tiles,))],
            cost=1,
        )
    else:
        stacked = jnp.concatenate(
            [obs_lateral, obs_vertical, jnp.broadcast_to(obs_weight[:, None], (moments, ROWS, slots))], axis=1
        )
        outgoing = stacked.reshape(moments, height, tiles, cap).transpose(2, 1, 0, 3).reshape(tiles, height, -1)

    halo = shape(((2 * moments - 1) * levels + ROWS, width), BF16)
    first, second = call(
        edges_kernel,
        [halo, halo],
        (neighbours, incr, costate, crossed),
        [ANY] * 4,
        scratch=[pltpu.VMEM(neighbours.shape, jnp.int32), semaphores, semaphores((4 * moments - 2,))],
        cost=1,
    )
    outgoing = gated(outgoing, first)
    first = exchanged(first, [(i, i + 1) for i in range(0, tiles - 1, 2)])
    second = exchanged(second, [(i, i + 1) for i in range(1, tiles - 1, 2)])
    arrived = lax.all_to_all(outgoing, "space", split_axis=0, concat_axis=0, tiled=True)
    if not packed:
        arrived = arrived.reshape(tiles, height, moments, cap).transpose(2, 1, 0, 3).reshape(moments, height, slots)

    pairs = (entries + 1) // 2
    inner = cols_all - 2 * width
    inner_residual, inner_base, *weights, target = call(
        interior_kernel,
        [shape((moments, levels, inner), BF16), shape((moments, levels, inner), F32)]
        + [shape((pairs, 2 * cols, 2 * cols), BF16)] * 2
        + [shape((levels, entries * levels), BF16)] * 2
        + [shape(obs_block.shape, jnp.int32)],
        (neighbours, obs_count, incr, costate, crossed, lateral_mix, vertical_mix, obs_block),
        [SMEM] * 2 + [VMEM] * 6,
        scratch=[pltpu.VMEM((moments, entries * levels, inner), BF16)],
        cost=4,
    )

    residual, *outer_base = call(
        edge_kernel,
        [shape(incr.shape, BF16)] + [shape((levels, 2 * width), F32)] * moments,
        (neighbours, incr, costate, crossed, first, second, *weights, inner_residual),
        [SMEM] + [VMEM] * 10,
        out_specs=[HBM] + [VMEM] * moments,
        scratch=[pltpu.VMEM(incr.shape, BF16)]
        + [pltpu.VMEM((moments, levels, 6 * width), BF16)] * 2
        + [pltpu.VMEM((moments, entries * levels, 2 * width), BF16), semaphores((moments,))],
        cost=4,
    )

    adjoint, image = call(
        functools.partial(observe_kernel, packed),
        [shape(incr.shape, BF16), shape((moments, slots), F32)],
        (incr, arrived, target, inner_base, *outer_base),
        [VMEM] * (4 + moments),
        out_specs=[HBM, HBM],
        scratch=[pltpu.VMEM(incr.shape, BF16), pltpu.VMEM((moments, slots), F32), semaphores((moments + 1,))],
        cost=3,
    )
    return residual, adjoint, image


def solution(mesh):
    fields = P(("groups", "tm"), None, "space")
    rows = P(("groups", "tm"), "space")
    in_specs = (
        fields, fields, P(), P(), P(("groups", "space"), None), fields, fields, rows, rows, rows,
    )
    return jax.shard_map(
        on_device, mesh=mesh, in_specs=in_specs, out_specs=(fields, fields, rows), check_vma=False
    )
```

```python
import functools

import jax
import jax.numpy as jnp
from jax import lax
from jax.experimental import pallas as pl
from jax.experimental.pallas import tpu as pltpu
from jax.sharding import PartitionSpec as P

REACH = 2
ROWS = 16
BF16 = jnp.bfloat16
F32 = jnp.float32
VMEM = pl.BlockSpec(memory_space=pltpu.VMEM)
ANY = pl.BlockSpec(memory_space=pl.ANY)
HBM = pl.BlockSpec(memory_space=pltpu.HBM)
SMEM = pl.BlockSpec(memory_space=pltpu.SMEM)


def dot(a, b):
    return jnp.dot(a, b, preferred_element_type=F32)


def dot_nt(a, b):
    return lax.dot_general(a, b, (((1,), (1,)), ((), ())), preferred_element_type=F32)


def exchanged(array, pairs):
    both = [(a, b) for a, b in pairs] + [(b, a) for a, b in pairs]
    return lax.ppermute(array, "space", both)


def call(kernel, out_shape, args, specs, out_specs=None, scratch=(), cost=0, limit=16, aliases=None):
    multiple = isinstance(out_shape, (list, tuple))
    return pl.pallas_call(
        kernel,
        out_shape=out_shape,
        in_specs=specs,
        out_specs=out_specs or ([VMEM] * len(out_shape) if multiple else VMEM),
        scratch_shapes=list(scratch),
        input_output_aliases=aliases or {},
        compiler_params=pltpu.CompilerParams(vmem_limit_bytes=limit * 1024 * 1024),
        cost_estimate=pl.CostEstimate(flops=cost * 1_000_000_000, bytes_accessed=cost * 1_000_000, transcendentals=0),
    )(*args)


def gated(data, after):
    return call(gate_kernel, jax.ShapeDtypeStruct(data.shape, BF16), (data, after), [ANY] * 2, ANY, limit=1, aliases={0: 0})


def fetched(pairs, sems):
    copies = [pltpu.make_async_copy(source, target, sems.at[k]) for k, (source, target) in enumerate(pairs)]
    for copy in copies:
        copy.start()
    return copies


def edges_kernel(near_any, incr, costate, crossed, first, second, near, near_sem, sems):
    moments, levels, cols = incr.shape
    blocks, entries = near.shape
    width = first.shape[1]
    place = lax.axis_index("space")
    odd = lax.rem(place, 2)
    fetch = pltpu.make_async_copy(near_any, near, near_sem)
    fetch.start()
    slabs = [incr.at[k] for k in range(moments - 1)] + [costate.at[k] for k in range(1, moments)] + [crossed]
    pairs = []
    for target, right in ((first, 1 - odd), (second, odd)):
        lanes = pl.ds(pl.multiple_of(right * (cols - width), 128), width)
        pairs += [(slab.at[:, lanes], target.at[pl.ds(k * levels, levels)]) for k, slab in enumerate(slabs)]
    copies = fetched(pairs, sems)
    fetch.wait()
    own = lax.broadcasted_iota(jnp.int32, near.shape, 0) + place * blocks
    distance = (near[...] - own).astype(F32)
    distance = distance.astype(BF16)
    for target in (first, second):
        target[len(slabs) * levels :] = jnp.zeros((blocks, width), BF16)
        target[len(slabs) * levels :, :entries] = distance
    for copy in copies:
        copy.wait()


def pack_kernel(obs_lateral, obs_vertical, obs_weight, out_any, out, out_sems):
    moments, cols, slots = obs_lateral.shape
    copies = []
    levels = obs_vertical.shape[1]
    tiles = out.shape[0]
    cap = slots // tiles
    for tile in range(tiles):
        lanes = slice(tile * cap, (tile + 1) * cap)
        out[tile, :cols] = jnp.concatenate([obs_lateral[s, :, lanes] for s in range(moments)], axis=1)
        out[tile, cols : cols + levels] = jnp.concatenate(
            [obs_vertical[s, :, lanes] for s in range(moments)], axis=1
        )
        row = jnp.concatenate([obs_weight[s : s + 1, lanes].astype(F32) for s in range(moments)], axis=1)
        out[tile, cols + levels :] = jnp.broadcast_to(row, (ROWS, row.shape[1])).astype(BF16)
        copies += fetched([(out.at[tile], out_any.at[tile])], out_sems.at[pl.ds(tile, 1)])
    for copy in copies:
        copy.wait()


def gate_kernel(data, after, out):
    pass


def mixed(get, moments, blocks, entries, pair, vert, stage):
    levels = vert.shape[0]
    cols = pair.shape[1] // 2
    for k in range((entries + 1) // 2):
        single = 2 * k + 1 >= entries
        weight = pair[k, :cols, :cols] if single else pair[k]
        rows = []
        for s in moments:
            for b in blocks:
                part = get(s, b, 2 * k)
                rows.append(part if single else jnp.concatenate([part, get(s, b, 2 * k + 1)], axis=1))
        result = dot(jnp.concatenate(rows, axis=0), weight).astype(BF16)
        for i, (s, n) in enumerate((s, n) for s in moments for n in range(len(blocks))):
            piece = result[i * levels : (i + 1) * levels]
            lanes = slice(n * cols, (n + 1) * cols)
            stage[s, 2 * k * levels : (2 * k + 1) * levels, lanes] = piece[:, :cols]
            if not single:
                stage[s, (2 * k + 1) * levels : (2 * k + 2) * levels, lanes] = piece[:, cols:]
    return [(s, dot(vert[...], stage[s])) for s in moments]


def interior_kernel(
    near, counts, incr, costate, crossed, lateral_mix, vertical_mix, owner,
    residual, base, pair_fwd, pair_bwd, vert_fwd, vert_bwd, target, stage,
):
    moments, levels, cols_all = incr.shape
    blocks, entries = near.shape
    cols = cols_all // blocks
    inner = list(range(REACH, blocks - REACH))
    lanes = slice(REACH * cols, (blocks - REACH) * cols)
    tm = lax.axis_index("tm")
    anchor = lax.axis_index("space") * blocks

    pair_fwd[...] = jnp.zeros(pair_fwd.shape, BF16)
    pair_bwd[...] = jnp.zeros(pair_bwd.shape, BF16)
    for j in range(entries):
        at = slice((j % 2) * cols, (j % 2 + 1) * cols)
        pair_fwd[j // 2, at, at] = lateral_mix[j]
        pair_bwd[j // 2, at, at] = lateral_mix[j].astype(F32).T.astype(BF16)
    vert_fwd[...] = jnp.concatenate([vertical_mix[j] for j in range(entries)], axis=1)
    vert_bwd[...] = jnp.concatenate([vertical_mix[j].astype(F32).T.astype(BF16) for j in range(entries)], axis=1)

    tiles = counts.shape[1]
    cap = owner.shape[1] // tiles
    slot = lax.broadcasted_iota(jnp.int32, (1, owner.shape[1]), 1)
    for s in range(moments):
        live = jnp.zeros(slot.shape, jnp.int32)
        for h in range(tiles):
            inside = (slot >= h * cap) & (slot < h * cap + counts[s, h])
            live = jnp.where(inside, 1, live)
        target[s : s + 1] = jnp.where(live == 1, owner[s : s + 1], -1)

    def forward(s, b, j):
        at = pl.ds(pl.multiple_of((near[b, j] - anchor) * cols, cols), cols)
        return crossed[:, at] if s == 0 else incr[s - 1, :, at]

    def backward(s, n, j):
        total = None
        for b in range(n - REACH, n + REACH + 1):
            at = slice(b * cols, (b + 1) * cols)
            source = crossed[:, at] if s == moments - 1 else costate[s + 1, :, at]
            term = jnp.where(near[b, j] == anchor + n, source, jnp.zeros_like(source)).astype(F32)
            total = term if total is None else total + term
        return total.astype(BF16)

    def run_forward(which):
        for s, pushed in mixed(forward, which, inner, entries, pair_fwd, vert_fwd, stage):
            residual[s] = (incr[s, :, lanes].astype(F32) - pushed).astype(BF16)

    def run_backward(which):
        for s, value in mixed(backward, which, inner, entries, pair_bwd, vert_bwd, stage):
            base[s] = costate[s, :, lanes].astype(F32) - value

    @pl.when(tm == 0)
    def _():
        residual[0] = incr[0, :, lanes]
        run_backward([moments - 1])

    @pl.when(tm == 1)
    def _():
        run_forward([0])
        base[moments - 1] = costate[moments - 1, :, lanes].astype(F32)

    run_forward(range(1, moments))
    run_backward(range(moments - 1))


def edge_kernel(
    near, incr, costate, crossed, first, second, pair_fwd, pair_bwd, vert_fwd, vert_bwd, inner_residual,
    residual_any, *rest,
):
    moments, levels, cols_all = incr.shape
    base = rest[:moments]
    residual, before, after, stage, sems = rest[moments:]
    blocks, entries = near.shape
    cols = cols_all // blocks
    width = REACH * cols
    place = lax.axis_index("space")
    odd = lax.rem(place, 2)
    tm = lax.axis_index("tm")
    anchor = place * blocks
    outer = [b for b in range(blocks) if b < REACH or b >= blocks - REACH]
    reach_cols = 3 * width

    def fill(target, s, source, edge):
        rows = slice(edge * levels, (edge + 1) * levels)
        one, two = first[rows], second[rows]
        target[s, :, :width] = jnp.where(odd == 1, one, two)
        target[s, :, width:reach_cols] = source[:, : 2 * width]
        target[s, :, reach_cols : reach_cols + 2 * width] = source[:, cols_all - 2 * width :]
        target[s, :, reach_cols + 2 * width :] = jnp.where(odd == 1, two, one)

    for s in range(moments - 1):
        fill(before, s + 1, incr[s], s)
        fill(after, s, costate[s + 1], moments - 1 + s)
    def forward(s, b, j):
        start = REACH if b < REACH else 5 * REACH - blocks
        at = pl.ds(pl.multiple_of((near[b, j] - anchor + start) * cols, cols), cols)
        return before[s, :, at]

    tail = slice((2 * moments - 1) * levels, (2 * moments - 1) * levels + blocks)
    one, two = first[tail, :cols].astype(F32), second[tail, :cols].astype(F32)
    left = jnp.where(odd == 1, one, two)
    right = jnp.where(odd == 1, two, one)

    def backward(s, n, j):
        total = None
        for b in range(n - REACH, n + REACH + 1):
            start = REACH if n < REACH else 5 * REACH - blocks
            source = after[s, :, (b + start) * cols : (b + start + 1) * cols]
            if 0 <= b < blocks:
                term = jnp.where(near[b, j] == anchor + n, source, jnp.zeros_like(source))
            else:
                row = b + blocks if b < 0 else b - blocks
                offset = (left if b < 0 else right)[row : row + 1, j : j + 1]
                hit = jnp.where(offset == float(n - b), 1.0, 0.0)
                term = source * jnp.broadcast_to(hit, source.shape).astype(BF16)
            total = term.astype(F32) if total is None else total + term.astype(F32)
        return total.astype(BF16)

    def ends(field, s):
        return jnp.concatenate([field[s, :, :width], field[s, :, cols_all - width :]], axis=1).astype(F32)

    def run_forward(which):
        for s, pushed in mixed(forward, which, outer, entries, pair_fwd, vert_fwd, stage):
            residual[s, :, :width] = (incr[s, :, :width].astype(F32) - pushed[:, :width]).astype(BF16)
            residual[s, :, width : cols_all - width] = inner_residual[s]
            residual[s, :, cols_all - width :] = (
                incr[s, :, cols_all - width :].astype(F32) - pushed[:, width:]
            ).astype(BF16)

    def run_backward(which):
        for s, value in mixed(backward, which, outer, entries, pair_bwd, vert_bwd, stage):
            base[s][...] = ends(costate, s) - value

    @pl.when(tm == 0)
    def _():
        residual[0] = incr[0]
        fill(after, moments - 1, crossed[...], 2 * (moments - 1))
        run_backward([moments - 1])

    @pl.when(tm == 1)
    def _():
        fill(before, 0, crossed[...], 2 * (moments - 1))
        run_forward([0])
        base[moments - 1][...] = ends(costate, moments - 1)

    run_forward(range(1, moments))
    copies = fetched([(residual.at[s], residual_any.at[s]) for s in range(moments)], sems)
    run_backward(range(moments - 1))
    for copy in copies:
        copy.wait()


def observe_kernel(packed, incr, arrived, target, inner_base, *rest):
    moments, levels, cols_all = incr.shape
    outer_base = rest[:moments]
    adjoint_any, image_any, adjoint, image, sems = rest[moments:]
    slots = target.shape[1]
    width = outer_base[0].shape[1] // 2
    cols = width // REACH
    blocks = cols_all // cols
    inner_lanes = slice(width, cols_all - width)
    copies = []
    for s in range(moments):
        block = target[s : s + 1]
        if packed:
            cap = arrived.shape[2] // moments
            part = slice(s * cap, (s + 1) * cap)
            whole = jnp.concatenate([arrived[h, :, part] for h in range(arrived.shape[0])], axis=1)
        else:
            whole = arrived[s]
        lateral = whole[:cols]
        vertical = whole[cols : cols + levels].astype(F32)
        weight = whole[cols + levels :].astype(F32)[:1]
        hits = [jnp.where(block == b, 1.0, 0.0) for b in range(blocks)]
        fields = jnp.concatenate([incr[s, :, b * cols : (b + 1) * cols] for b in range(blocks)], axis=0)
        seen = dot(fields, lateral)
        along = sum(hits[b] * seen[b * levels : (b + 1) * levels] for b in range(blocks))
        image[s : s + 1] = jnp.sum(vertical * along, axis=0, keepdims=True)
        if s == moments - 1:
            copies += fetched([(image, image_any)], sems.at[pl.ds(moments, 1)])
        scaled = (vertical * weight).astype(BF16)
        parts = [scaled * jnp.broadcast_to(hit, scaled.shape).astype(BF16) for hit in hits]
        stacked = dot_nt(jnp.concatenate(parts, axis=0), lateral)
        push = jnp.concatenate([stacked[b * levels : (b + 1) * levels] for b in range(blocks)], axis=1)
        adjoint[s, :, :width] = (outer_base[s][:, :width] + push[:, :width]).astype(BF16)
        adjoint[s, :, inner_lanes] = (inner_base[s] + push[:, inner_lanes]).astype(BF16)
        adjoint[s, :, cols_all - width :] = (outer_base[s][:, width:] + push[:, cols_all - width :]).astype(BF16)
        copies += fetched([(adjoint.at[s], adjoint_any.at[s])], sems.at[pl.ds(s, 1)])
    for copy in copies:
        copy.wait()


def on_device(
    incr, costate, lateral_mix, vertical_mix, neighbours,
    obs_lateral, obs_vertical, obs_weight, obs_block, obs_count,
):
    moments, levels, cols_all = incr.shape
    entries, cols, _ = lateral_mix.shape
    blocks = neighbours.shape[0]
    slots = obs_block.shape[1]
    tiles = lax.axis_size("space")
    cap = slots // tiles
    width = REACH * cols
    tm = lax.axis_index("tm")
    shape = jax.ShapeDtypeStruct
    semaphores = pltpu.SemaphoreType.DMA

    crossed = lax.ppermute(jnp.where(tm == 0, incr[-1], costate[0]), "tm", [(0, 1), (1, 0)])

    height = cols + levels + ROWS
    packed = moments * cap == 128
    if packed:
        outgoing = call(
            pack_kernel,
            shape((tiles, height, moments * cap), BF16),
            (obs_lateral, obs_vertical, obs_weight),
            [VMEM] * 3,
            out_specs=HBM,
            scratch=[pltpu.VMEM((tiles, height, moments * cap), BF16), semaphores((tiles,))],
            cost=1,
        )
    else:
        stacked = jnp.concatenate(
            [obs_lateral, obs_vertical, jnp.broadcast_to(obs_weight[:, None], (moments, ROWS, slots))], axis=1
        )
        outgoing = stacked.reshape(moments, height, tiles, cap).transpose(2, 1, 0, 3).reshape(tiles, height, -1)

    halo = shape(((2 * moments - 1) * levels + blocks, width), BF16)
    first, second = call(
        edges_kernel,
        [halo, halo],
        (neighbours, incr, costate, crossed),
        [ANY] * 4,
        scratch=[pltpu.VMEM(neighbours.shape, jnp.int32), semaphores, semaphores((4 * moments - 2,))],
        cost=1,
    )
    outgoing = gated(outgoing, first)
    first = exchanged(first, [(i, i + 1) for i in range(0, tiles - 1, 2)])
    second = exchanged(second, [(i, i + 1) for i in range(1, tiles - 1, 2)])
    arrived = lax.all_to_all(outgoing, "space", split_axis=0, concat_axis=0, tiled=True)
    if not packed:
        arrived = arrived.reshape(tiles, height, moments, cap).transpose(2, 1, 0, 3).reshape(moments, height, slots)

    pairs = (entries + 1) // 2
    inner = cols_all - 2 * width
    inner_residual, inner_base, *weights, target = call(
        interior_kernel,
        [shape((moments, levels, inner), BF16), shape((moments, levels, inner), F32)]
        + [shape((pairs, 2 * cols, 2 * cols), BF16)] * 2
        + [shape((levels, entries * levels), BF16)] * 2
        + [shape(obs_block.shape, jnp.int32)],
        (neighbours, obs_count, incr, costate, crossed, lateral_mix, vertical_mix, obs_block),
        [SMEM] * 2 + [VMEM] * 6,
        scratch=[pltpu.VMEM((moments, entries * levels, inner), BF16)],
        cost=4,
    )

    residual, *outer_base = call(
        edge_kernel,
        [shape(incr.shape, BF16)] + [shape((levels, 2 * width), F32)] * moments,
        (neighbours, incr, costate, crossed, first, second, *weights, inner_residual),
        [SMEM] + [VMEM] * 10,
        out_specs=[HBM] + [VMEM] * moments,
        scratch=[pltpu.VMEM(incr.shape, BF16)]
        + [pltpu.VMEM((moments, levels, 6 * width), BF16)] * 2
        + [pltpu.VMEM((moments, entries * levels, 2 * width), BF16), semaphores((moments,))],
        cost=4,
    )

    adjoint, image = call(
        functools.partial(observe_kernel, packed),
        [shape(incr.shape, BF16), shape((moments, slots), F32)],
        (incr, arrived, target, inner_base, *outer_base),
        [VMEM] * (4 + moments),
        out_specs=[HBM, HBM],
        scratch=[pltpu.VMEM(incr.shape, BF16), pltpu.VMEM((moments, slots), F32), semaphores((moments + 1,))],
        cost=3,
    )
    return residual, adjoint, image


def solution(mesh):
    fields = P(("groups", "tm"), None, "space")
    rows = P(("groups", "tm"), "space")
    in_specs = (
        fields, fields, P(), P(), P(("groups", "space"), None), fields, fields, rows, rows, rows,
    )
    return jax.shard_map(
        on_device, mesh=mesh, in_specs=in_specs, out_specs=(fields, fields, rows), check_vma=False
    )
```

```python
import functools

import jax
import jax.numpy as jnp
from jax import lax
from jax.experimental import pallas as pl
from jax.experimental.pallas import tpu as pltpu
from jax.sharding import PartitionSpec as P

REACH = 2
ROWS = 16
BF16 = jnp.bfloat16
F32 = jnp.float32
VMEM = pl.BlockSpec(memory_space=pltpu.VMEM)
ANY = pl.BlockSpec(memory_space=pl.ANY)
HBM = pl.BlockSpec(memory_space=pltpu.HBM)
SMEM = pl.BlockSpec(memory_space=pltpu.SMEM)


def dot(a, b):
    return jnp.dot(a, b, preferred_element_type=F32)


def dot_nt(a, b):
    return lax.dot_general(a, b, (((1,), (1,)), ((), ())), preferred_element_type=F32)


def exchanged(array, pairs):
    both = [(a, b) for a, b in pairs] + [(b, a) for a, b in pairs]
    return lax.ppermute(array, "space", both)


def call(kernel, out_shape, args, specs, out_specs=None, scratch=(), cost=0, limit=16, aliases=None):
    multiple = isinstance(out_shape, (list, tuple))
    return pl.pallas_call(
        kernel,
        out_shape=out_shape,
        in_specs=specs,
        out_specs=out_specs or ([VMEM] * len(out_shape) if multiple else VMEM),
        scratch_shapes=list(scratch),
        input_output_aliases=aliases or {},
        compiler_params=pltpu.CompilerParams(vmem_limit_bytes=limit * 1024 * 1024),
        cost_estimate=pl.CostEstimate(flops=cost * 1_000_000_000, bytes_accessed=cost * 1_000_000, transcendentals=0),
    )(*args)


def gated(data, after):
    return call(gate_kernel, jax.ShapeDtypeStruct(data.shape, BF16), (data, after), [ANY] * 2, ANY, limit=1, aliases={0: 0})


def fetched(pairs, sems):
    copies = [pltpu.make_async_copy(source, target, sems.at[k]) for k, (source, target) in enumerate(pairs)]
    for copy in copies:
        copy.start()
    return copies


def edges_kernel(near_any, incr, costate, crossed, first, second, near, near_sem, sems):
    moments, levels, cols = incr.shape
    blocks, entries = near.shape
    width = first.shape[1]
    place = lax.axis_index("space")
    odd = lax.rem(place, 2)
    fetch = pltpu.make_async_copy(near_any, near, near_sem)
    fetch.start()
    slabs = [incr.at[k] for k in range(moments - 1)] + [costate.at[k] for k in range(1, moments)] + [crossed]
    pairs = []
    for target, right in ((first, 1 - odd), (second, odd)):
        lanes = pl.ds(pl.multiple_of(right * (cols - width), 128), width)
        pairs += [(slab.at[:, lanes], target.at[pl.ds(k * levels, levels)]) for k, slab in enumerate(slabs)]
    copies = fetched(pairs, sems)
    fetch.wait()
    own = lax.broadcasted_iota(jnp.int32, near.shape, 0) + place * blocks
    distance = (near[...] - own).astype(F32)
    distance = jnp.concatenate([distance, jnp.zeros((ROWS - blocks, entries), F32)], axis=0).astype(BF16)
    for target in (first, second):
        target[len(slabs) * levels :] = jnp.zeros((ROWS, width), BF16)
        target[len(slabs) * levels :, :entries] = distance
    for copy in copies:
        copy.wait()


def pack_kernel(obs_lateral, obs_vertical, obs_weight, out_any, out, out_sems):
    moments, cols, slots = obs_lateral.shape
    copies = []
    levels = obs_vertical.shape[1]
    tiles = out.shape[0]
    cap = slots // tiles
    for tile in range(tiles):
        lanes = slice(tile * cap, (tile + 1) * cap)
        out[tile, :cols] = jnp.concatenate([obs_lateral[s, :, lanes] for s in range(moments)], axis=1)
        out[tile, cols : cols + levels] = jnp.concatenate(
            [obs_vertical[s, :, lanes] for s in range(moments)], axis=1
        )
        row = jnp.concatenate([obs_weight[s : s + 1, lanes].astype(F32) for s in range(moments)], axis=1)
        out[tile, cols + levels :] = jnp.broadcast_to(row, (ROWS, row.shape[1])).astype(BF16)
        copies += fetched([(out.at[tile], out_any.at[tile])], out_sems.at[pl.ds(tile, 1)])
    for copy in copies:
        copy.wait()


def gate_kernel(data, after, out):
    pass


def mixed(get, moments, blocks, entries, pair, vert, stage):
    levels = vert.shape[0]
    cols = pair.shape[1] // 2
    for k in range((entries + 1) // 2):
        single = 2 * k + 1 >= entries
        weight = pair[k, :cols, :cols] if single else pair[k]
        rows = []
        for s in moments:
            for b in blocks:
                part = get(s, b, 2 * k)
                rows.append(part if single else jnp.concatenate([part, get(s, b, 2 * k + 1)], axis=1))
        result = dot(jnp.concatenate(rows, axis=0), weight).astype(BF16)
        for i, (s, n) in enumerate((s, n) for s in moments for n in range(len(blocks))):
            piece = result[i * levels : (i + 1) * levels]
            lanes = slice(n * cols, (n + 1) * cols)
            stage[s, 2 * k * levels : (2 * k + 1) * levels, lanes] = piece[:, :cols]
            if not single:
                stage[s, (2 * k + 1) * levels : (2 * k + 2) * levels, lanes] = piece[:, cols:]
    return [(s, dot(vert[...], stage[s])) for s in moments]


def interior_kernel(
    near, counts, incr, costate, crossed, lateral_mix, vertical_mix, owner,
    residual, base, pair_fwd, pair_bwd, vert_fwd, vert_bwd, target, stage,
):
    moments, levels, cols_all = incr.shape
    blocks, entries = near.shape
    cols = cols_all // blocks
    inner = list(range(REACH, blocks - REACH))
    lanes = slice(REACH * cols, (blocks - REACH) * cols)
    tm = lax.axis_index("tm")
    anchor = lax.axis_index("space") * blocks

    pair_fwd[...] = jnp.zeros(pair_fwd.shape, BF16)
    pair_bwd[...] = jnp.zeros(pair_bwd.shape, BF16)
    for j in range(entries):
        at = slice((j % 2) * cols, (j % 2 + 1) * cols)
        pair_fwd[j // 2, at, at] = lateral_mix[j]
        pair_bwd[j // 2, at, at] = lateral_mix[j].astype(F32).T.astype(BF16)
    vert_fwd[...] = jnp.concatenate([vertical_mix[j] for j in range(entries)], axis=1)
    vert_bwd[...] = jnp.concatenate([vertical_mix[j].astype(F32).T.astype(BF16) for j in range(entries)], axis=1)

    tiles = counts.shape[1]
    cap = owner.shape[1] // tiles
    slot = lax.broadcasted_iota(jnp.int32, (1, owner.shape[1]), 1)
    for s in range(moments):
        live = jnp.zeros(slot.shape, jnp.int32)
        for h in range(tiles):
            inside = (slot >= h * cap) & (slot < h * cap + counts[s, h])
            live = jnp.where(inside, 1, live)
        target[s : s + 1] = jnp.where(live == 1, owner[s : s + 1], -1)

    def forward(s, b, j):
        at = pl.ds(pl.multiple_of((near[b, j] - anchor) * cols, cols), cols)
        return crossed[:, at] if s == 0 else incr[s - 1, :, at]

    def backward(s, n, j):
        total = None
        for b in range(n - REACH, n + REACH + 1):
            at = slice(b * cols, (b + 1) * cols)
            source = crossed[:, at] if s == moments - 1 else costate[s + 1, :, at]
            term = jnp.where(near[b, j] == anchor + n, source, jnp.zeros_like(source)).astype(F32)
            total = term if total is None else total + term
        return total.astype(BF16)

    def run_forward(which):
        for s, pushed in mixed(forward, which, inner, entries, pair_fwd, vert_fwd, stage):
            residual[s] = (incr[s, :, lanes].astype(F32) - pushed).astype(BF16)

    def run_backward(which):
        for s, value in mixed(backward, which, inner, entries, pair_bwd, vert_bwd, stage):
            base[s] = costate[s, :, lanes].astype(F32) - value

    @pl.when(tm == 0)
    def _():
        residual[0] = incr[0, :, lanes]
        run_backward([moments - 1])

    @pl.when(tm == 1)
    def _():
        run_forward([0])
        base[moments - 1] = costate[moments - 1, :, lanes].astype(F32)

    run_forward(range(1, moments))
    run_backward(range(moments - 1))


def edge_kernel(
    near, incr, costate, crossed, first, second, pair_fwd, pair_bwd, vert_fwd, vert_bwd, inner_residual,
    residual_any, *rest,
):
    moments, levels, cols_all = incr.shape
    base = rest[:moments]
    residual, before, after, stage, sems = rest[moments:]
    blocks, entries = near.shape
    cols = cols_all // blocks
    width = REACH * cols
    place = lax.axis_index("space")
    odd = lax.rem(place, 2)
    tm = lax.axis_index("tm")
    anchor = place * blocks
    outer = [b for b in range(blocks) if b < REACH or b >= blocks - REACH]
    reach_cols = 3 * width

    def fill(target, s, source, edge):
        rows = slice(edge * levels, (edge + 1) * levels)
        one, two = first[rows], second[rows]
        target[s, :, :width] = jnp.where(odd == 1, one, two)
        target[s, :, width:reach_cols] = source[:, : 2 * width]
        target[s, :, reach_cols : reach_cols + 2 * width] = source[:, cols_all - 2 * width :]
        target[s, :, reach_cols + 2 * width :] = jnp.where(odd == 1, two, one)

    for s in range(moments - 1):
        fill(before, s + 1, incr[s], s)
        fill(after, s, costate[s + 1], moments - 1 + s)
    def forward(s, b, j):
        start = REACH if b < REACH else 5 * REACH - blocks
        at = pl.ds(pl.multiple_of((near[b, j] - anchor + start) * cols, cols), cols)
        return before[s, :, at]

    tail = slice((2 * moments - 1) * levels, (2 * moments - 1) * levels + ROWS)
    one, two = first[tail, :cols].astype(F32), second[tail, :cols].astype(F32)
    left = jnp.where(odd == 1, one, two)
    right = jnp.where(odd == 1, two, one)

    def backward(s, n, j):
        total = None
        for b in range(n - REACH, n + REACH + 1):
            start = REACH if n < REACH else 5 * REACH - blocks
            source = after[s, :, (b + start) * cols : (b + start + 1) * cols]
            if 0 <= b < blocks:
                term = jnp.where(near[b, j] == anchor + n, source, jnp.zeros_like(source))
            else:
                row = b + blocks if b < 0 else b - blocks
                offset = (left if b < 0 else right)[row : row + 1, j : j + 1]
                hit = jnp.where(offset == float(n - b), 1.0, 0.0)
                term = source * jnp.broadcast_to(hit, source.shape).astype(BF16)
            total = term.astype(F32) if total is None else total + term.astype(F32)
        return total.astype(BF16)

    def ends(field, s):
        return jnp.concatenate([field[s, :, :width], field[s, :, cols_all - width :]], axis=1).astype(F32)

    def run_forward(which):
        for s, pushed in mixed(forward, which, outer, entries, pair_fwd, vert_fwd, stage):
            residual[s, :, :width] = (incr[s, :, :width].astype(F32) - pushed[:, :width]).astype(BF16)
            residual[s, :, width : cols_all - width] = inner_residual[s]
            residual[s, :, cols_all - width :] = (
                incr[s, :, cols_all - width :].astype(F32) - pushed[:, width:]
            ).astype(BF16)

    def run_backward(which):
        for s, value in mixed(backward, which, outer, entries, pair_bwd, vert_bwd, stage):
            base[s][...] = ends(costate, s) - value

    @pl.when(tm == 0)
    def _():
        residual[0] = incr[0]
        fill(after, moments - 1, crossed[...], 2 * (moments - 1))
        run_backward([moments - 1])

    @pl.when(tm == 1)
    def _():
        fill(before, 0, crossed[...], 2 * (moments - 1))
        run_forward([0])
        base[moments - 1][...] = ends(costate, moments - 1)

    run_forward(range(1, moments))
    copies = fetched([(residual.at[s], residual_any.at[s]) for s in range(moments)], sems)
    run_backward(range(moments - 1))
    for copy in copies:
        copy.wait()


def observe_kernel(packed, incr, arrived, target, inner_base, *rest):
    moments, levels, cols_all = incr.shape
    outer_base = rest[:moments]
    adjoint_any, image_any, adjoint, image, sems = rest[moments:]
    slots = target.shape[1]
    width = outer_base[0].shape[1] // 2
    cols = width // REACH
    blocks = cols_all // cols
    inner_lanes = slice(width, cols_all - width)
    copies = []
    for s in range(moments):
        block = target[s : s + 1]
        if packed:
            cap = arrived.shape[2] // moments
            part = slice(s * cap, (s + 1) * cap)
            whole = jnp.concatenate([arrived[h, :, part] for h in range(arrived.shape[0])], axis=1)
        else:
            whole = arrived[s]
        lateral = whole[:cols]
        vertical = whole[cols : cols + levels].astype(F32)
        weight = whole[cols + levels :].astype(F32)[:1]
        hits = [jnp.where(block == b, 1.0, 0.0) for b in range(blocks)]
        scaled = (vertical * weight).astype(BF16)
        parts = [scaled * jnp.broadcast_to(hit, scaled.shape).astype(BF16) for hit in hits]
        stacked = dot_nt(jnp.concatenate(parts, axis=0), lateral)
        push = jnp.concatenate([stacked[b * levels : (b + 1) * levels] for b in range(blocks)], axis=1)
        adjoint[s, :, :width] = (outer_base[s][:, :width] + push[:, :width]).astype(BF16)
        adjoint[s, :, inner_lanes] = (inner_base[s] + push[:, inner_lanes]).astype(BF16)
        adjoint[s, :, cols_all - width :] = (outer_base[s][:, width:] + push[:, cols_all - width :]).astype(BF16)
        copies += fetched([(adjoint.at[s], adjoint_any.at[s])], sems.at[pl.ds(s, 1)])
        fields = jnp.concatenate([incr[s, :, b * cols : (b + 1) * cols] for b in range(blocks)], axis=0)
        seen = dot(fields, lateral)
        along = sum(hits[b] * seen[b * levels : (b + 1) * levels] for b in range(blocks))
        image[s : s + 1] = jnp.sum(vertical * along, axis=0, keepdims=True)
        if s == moments - 1:
            copies += fetched([(image, image_any)], sems.at[pl.ds(moments, 1)])
    for copy in copies:
        copy.wait()


def on_device(
    incr, costate, lateral_mix, vertical_mix, neighbours,
    obs_lateral, obs_vertical, obs_weight, obs_block, obs_count,
):
    moments, levels, cols_all = incr.shape
    entries, cols, _ = lateral_mix.shape
    blocks = neighbours.shape[0]
    slots = obs_block.shape[1]
    tiles = lax.axis_size("space")
    cap = slots // tiles
    width = REACH * cols
    tm = lax.axis_index("tm")
    shape = jax.ShapeDtypeStruct
    semaphores = pltpu.SemaphoreType.DMA

    crossed = lax.ppermute(jnp.where(tm == 0, incr[-1], costate[0]), "tm", [(0, 1), (1, 0)])

    height = cols + levels + ROWS
    packed = moments * cap == 128
    if packed:
        outgoing = call(
            pack_kernel,
            shape((tiles, height, moments * cap), BF16),
            (obs_lateral, obs_vertical, obs_weight),
            [VMEM] * 3,
            out_specs=HBM,
            scratch=[pltpu.VMEM((tiles, height, moments * cap), BF16), semaphores((tiles,))],
            cost=1,
        )
    else:
        stacked = jnp.concatenate(
            [obs_lateral, obs_vertical, jnp.broadcast_to(obs_weight[:, None], (moments, ROWS, slots))], axis=1
        )
        outgoing = stacked.reshape(moments, height, tiles, cap).transpose(2, 1, 0, 3).reshape(tiles, height, -1)

    halo = shape(((2 * moments - 1) * levels + ROWS, width), BF16)
    first, second = call(
        edges_kernel,
        [halo, halo],
        (neighbours, incr, costate, crossed),
        [ANY] * 4,
        scratch=[pltpu.VMEM(neighbours.shape, jnp.int32), semaphores, semaphores((4 * moments - 2,))],
        cost=1,
    )
    outgoing = gated(outgoing, first)
    first = exchanged(first, [(i, i + 1) for i in range(0, tiles - 1, 2)])
    second = exchanged(second, [(i, i + 1) for i in range(1, tiles - 1, 2)])
    arrived = lax.all_to_all(outgoing, "space", split_axis=0, concat_axis=0, tiled=True)
    if not packed:
        arrived = arrived.reshape(tiles, height, moments, cap).transpose(2, 1, 0, 3).reshape(moments, height, slots)

    pairs = (entries + 1) // 2
    inner = cols_all - 2 * width
    inner_residual, inner_base, *weights, target = call(
        interior_kernel,
        [shape((moments, levels, inner), BF16), shape((moments, levels, inner), F32)]
        + [shape((pairs, 2 * cols, 2 * cols), BF16)] * 2
        + [shape((levels, entries * levels), BF16)] * 2
        + [shape(obs_block.shape, jnp.int32)],
        (neighbours, obs_count, incr, costate, crossed, lateral_mix, vertical_mix, obs_block),
        [SMEM] * 2 + [VMEM] * 6,
        scratch=[pltpu.VMEM((moments, entries * levels, inner), BF16)],
        cost=4,
    )

    residual, *outer_base = call(
        edge_kernel,
        [shape(incr.shape, BF16)] + [shape((levels, 2 * width), F32)] * moments,
        (neighbours, incr, costate, crossed, first, second, *weights, inner_residual),
        [SMEM] + [VMEM] * 10,
        out_specs=[HBM] + [VMEM] * moments,
        scratch=[pltpu.VMEM(incr.shape, BF16)]
        + [pltpu.VMEM((moments, levels, 6 * width), BF16)] * 2
        + [pltpu.VMEM((moments, entries * levels, 2 * width), BF16), semaphores((moments,))],
        cost=4,
    )

    adjoint, image = call(
        functools.partial(observe_kernel, packed),
        [shape(incr.shape, BF16), shape((moments, slots), F32)],
        (incr, arrived, target, inner_base, *outer_base),
        [VMEM] * (4 + moments),
        out_specs=[HBM, HBM],
        scratch=[pltpu.VMEM(incr.shape, BF16), pltpu.VMEM((moments, slots), F32), semaphores((moments + 1,))],
        cost=3,
    )
    return residual, adjoint, image


def solution(mesh):
    fields = P(("groups", "tm"), None, "space")
    rows = P(("groups", "tm"), "space")
    in_specs = (
        fields, fields, P(), P(), P(("groups", "space"), None), fields, fields, rows, rows, rows,
    )
    return jax.shard_map(
        on_device, mesh=mesh, in_specs=in_specs, out_specs=(fields, fields, rows), check_vma=False
    )
```
